128 devices in a mesh: seq: 16 (over y, z), head: 8 (over x, core).
Axes of the slice: x: 4, y: 4, z: 4, core: 2. Of those that a mesh axis runs over, the one named last changes fastest.
Arguments:
- inputs: bfloat16 [32768, 16384], P('seq', 'head'), may hold values from -6 to 6
- gates: bfloat16 [32768, 16384], P('seq', 'head'), may hold values from -6 to 6
- writes: bfloat16 [32768, 1024], P('seq', 'head'), may hold values from -2 to 2
- reads: bfloat16 [32768, 1024], P('seq', 'head'), may hold values from -2 to 2
- step_raw: float32 [128, 32768], P('head', 'seq'), may hold values from -3 to 3
- step_bias: float32 [128], P('head'), may hold values from -1 to 1
- decay_rate: float32 [128], P('head'), may hold values from 3e-05 to 0.06
- skip_gain: float32 [128], P('head'), may hold values from 0.5 to 2
- conv_inputs: bfloat16 [4, 16384], P(None, 'head'), may hold values from -3 to 3
- conv_writes: bfloat16 [4, 1024], P(None, 'head'), may hold values from -3 to 3
- conv_reads: bfloat16 [4, 1024], P(None, 'head'), may hold values from -3 to 3
- norm_gain: float32 [16384], P('head'), may hold values from 0.1 to 1.9
- positions: int32 [32768], P('seq'), may hold values from 0 to 32767, as said below
- segments: int32 [32768], replicated, may hold values from 0 to 5, never falling along the last dimension, each value on 1 to 10922 neighbouring positions
Outputs:
- outputs: bfloat16 [32768, 16384], P('seq', 'head')
The draws below stay inside these ranges and needn't reach their ends.
Inputs may be any that keep to these rules, and one draw needn't show every extreme that they name: The rows of seq shard i are the positions of two blocks of 1024 positions each: block i and block 31 - i of the sequence, each in increasing order, the two blocks in either order. `segments`: never falling along the positions; each value is one document.
All inputs are finite; a program needn't handle non-finite values.
Results may differ from the reference program's by a relative error of at most 0.0065.
Values may be sent and summed in bfloat16 or wider, within the bound.
A program may use at most 256 MiB of HBM per device.

```python
import math
import jax
import jax.numpy as jnp
import numpy as np
from jax import lax

H = 128
P_SIZE = 128
N = 128
G = 8
BLOCK = 512
HALF = 1024
TOKENS = 32768
N_SEQ = 16


def draw_positions(key, part):
    key = jax.random.fold_in(key, 11)
    flips = jax.random.randint(key, (N_SEQ,), 0, 2)
    device_ids = jnp.arange(N_SEQ, dtype=jnp.int32)
    low_start = device_ids * HALF
    high_start = (2 * N_SEQ - 1 - device_ids) * HALF
    first_start = jnp.where(flips == 1, high_start, low_start)
    second_start = jnp.where(flips == 1, low_start, high_start)
    offsets = jnp.arange(HALF, dtype=jnp.int32)
    joined = jnp.concatenate([first_start[:, None] + offsets[None, :], second_start[:, None] + offsets[None, :]], axis=1)
    return joined.reshape(-1).astype(jnp.int32)


def level_of(key, dims, split, least, top_value):
    level = 1.0
    for axis_at, blocks in split:
        heights = jax.random.uniform(jax.random.fold_in(jax.random.fold_in(key, 6), axis_at), (blocks,), jnp.float32, least / len(split), top_value / len(split))
        level = level * jnp.repeat(jnp.exp(heights), dims[axis_at] // blocks).reshape((-1,) + (1,) * (len(dims) - 1 - axis_at))
    return level


def profile(number_of, total, most, lean):
    weights = [(1 << 20) // math.isqrt(grade ** lean) + 1 for grade in range(2, number_of + 1)]
    rest, given = total - most - (number_of - 1), [1] * (number_of - 1)
    while rest > 0:
        movable = [i for i in range(number_of - 1) if given[i] < most]
        whole, left = sum([weights[i] for i in movable]), rest
        for i in movable:
            more = min(most - given[i], max(1, left * weights[i] // whole), rest)
            given[i] = given[i] + more
            rest = rest - more
    return np.array([most] + given)


def uneven_parts(rng, amount, total, most, slope):
    if amount == 2:
        one = jax.random.randint(rng, (), max(1, total - most), min(most, total - 1) + 1)
        return jnp.stack([one, total - one])
    sizes = jnp.asarray(profile(amount, total, most, slope), jnp.int32)
    twos = (amount - 1) // 2
    donor, sink = sizes[1:1 + 2 * twos:2], sizes[2:2 + 2 * twos:2]
    room = jnp.minimum(donor - 1, most - sink)
    shifted = jax.random.randint(jax.random.fold_in(rng, 1), (twos,), 0, 1 << 20) % (room + 1)
    sizes = sizes.at[1:1 + 2 * twos:2].set(donor - shifted).at[2:2 + 2 * twos:2].set(sink + shifted)
    return sizes[jax.random.permutation(jax.random.fold_in(rng, 2), amount)]


def bell_draw(stream_key, shape, deviation, limit, split=(), kind=jnp.bfloat16):
    result = jax.random.normal(stream_key, shape, jnp.float32) * deviation
    if len(split) > 0:
        result = level_of(stream_key, shape, split, -0.22, 0.18) * result
    return jnp.clip(result, min=-limit, max=limit).astype(kind)


def setup_inputs(seed: int = 0) -> dict:
    key_of = jax.random.split(jax.random.key(seed), 15)
    inputs = bell_draw(key_of[0], (TOKENS, H * P_SIZE), 1.0, 6.0, ((0, 16), (1, 8)))
    gates = bell_draw(key_of[1], (TOKENS, H * P_SIZE), 1.0, 6.0, ((0, 16), (1, 8)))
    writes = bell_draw(key_of[2], (TOKENS, G * N), 0.3, 2.0, ((0, 16), (1, 8)))
    reads = bell_draw(key_of[3], (TOKENS, G * N), 0.3, 2.0, ((0, 16), (1, 8)))
    step_raw = bell_draw(key_of[4], (H, TOKENS), 0.5, 3.0, ((0, 8), (1, 16)), jnp.float32)
    step_bias = jnp.clip(jax.random.uniform(key_of[5], (H,), jnp.float32, -1.0, 1.0) * level_of(key_of[5], (H,), ((0, 8),), -0.4, 0.0), -1.0, 1.0)
    decay_rate = jnp.clip(jnp.exp(math.log(0.06) - 7.6009025 * jax.random.uniform(key_of[6], (H,), jnp.float32) ** level_of(key_of[6], (H,), ((0, 8),), -0.2, 0.2)), 2.9999999242136255e-05, 0.06)
    skip_gain = jnp.clip(0.5 + 1.5 * jax.random.uniform(key_of[7], (H,), jnp.float32) ** level_of(key_of[7], (H,), ((0, 8),), -0.2, 0.2), 0.5, 2.0)
    conv_inputs = bell_draw(key_of[8], (4, H * P_SIZE), 4 ** -0.5, 3.0, ((1, 8),))
    conv_writes = bell_draw(key_of[9], (4, G * N), 4 ** -0.5, 3.0, ((1, 8),))
    conv_reads = bell_draw(key_of[10], (4, G * N), 4 ** -0.5, 3.0, ((1, 8),))
    norm_gain = jnp.clip(1.0 + 0.18 * jax.random.normal(key_of[11], (H * P_SIZE,), jnp.float32), 0.1, 1.9)
    positions = draw_positions(jax.random.fold_in(key_of[14], 71), 0)
    segments = jnp.searchsorted(jnp.cumsum(uneven_parts(key_of[13], 6, TOKENS, TOKENS // 3, 0)), jnp.arange(TOKENS), side="right").astype(jnp.int32)
    return dict(inputs=inputs, gates=gates, writes=writes, reads=reads, step_raw=step_raw, step_bias=step_bias, decay_rate=decay_rate, skip_gain=skip_gain, conv_inputs=conv_inputs, conv_writes=conv_writes, conv_reads=conv_reads, norm_gain=norm_gain, positions=positions, segments=segments)


EPSILON = 1e-05

def convolve(window, taps, seg_window):
    length = window.shape[0] - 3
    summed = jnp.zeros((length, window.shape[1]), jnp.float32)
    for k in range(4):
        same_doc = (seg_window[k:k + length] == seg_window[3:])[:, None]
        term = window[k:k + length].astype(jnp.float32) * taps[k].astype(jnp.float32)
        summed = summed + jnp.where(same_doc, term, 0.0)
    return jax.nn.silu(summed).astype(jnp.bfloat16)

def block_parts(features, writes, reads, step_size, log_decay, seg_block, seg_before):
    length = features.shape[0]
    scores = jnp.einsum('tgn,sgn->gts', reads.astype(jnp.float32), writes.astype(jnp.float32))
    cumulative = jnp.cumsum(log_decay, axis=2)
    spread = cumulative[:, :, :, None] - cumulative[:, :, None, :]
    indices = jnp.arange(length, dtype=jnp.int32)
    same_doc = (seg_block[:, None] == seg_block[None, :]) & (indices[None, :] <= indices[:, None])
    decay_mask = jnp.where(same_doc, jnp.exp(jnp.minimum(spread, 0.0)), 0.0)
    weights = (scores[:, None] * decay_mask * step_size[:, :, None, :]).astype(jnp.bfloat16)
    inner_part = jnp.einsum('gets,sgep->tgep', weights.astype(jnp.float32), features.astype(jnp.float32))
    keep_end = seg_block == seg_block[length - 1]
    tail_scale = jnp.where(keep_end, jnp.exp(cumulative[:, :, length - 1:] - cumulative) * step_size, 0.0)
    write_scaled = (jnp.transpose(writes, (1, 0, 2)).astype(jnp.float32)[:, None] * tail_scale[..., None]).astype(jnp.bfloat16)
    state_add = jnp.einsum('sgep,gesn->gepn', features.astype(jnp.float32), write_scaled.astype(jnp.float32))
    block_decay = jnp.where(seg_block[length - 1] == seg_before, jnp.exp(cumulative[:, :, length - 1]), 0.0)
    return (inner_part, state_add, block_decay, cumulative)

def block_inter(reads, cumulative, seg_block, seg_before, state_in):
    enter_mask = seg_block == seg_before
    read_scaled = (jnp.transpose(reads, (1, 0, 2)).astype(jnp.float32)[:, None] * jnp.where(enter_mask, jnp.exp(cumulative), 0.0)[..., None]).astype(jnp.bfloat16)
    state_low = state_in.astype(jnp.bfloat16)
    return jnp.einsum('gein,gepn->igep', read_scaled.astype(jnp.float32), state_low.astype(jnp.float32))

def reference(inputs, gates, writes, reads, step_raw, step_bias, decay_rate, skip_gain, conv_inputs, conv_writes, conv_reads, norm_gain, positions, segments):
    per_group = H // G
    inverse = jnp.zeros((TOKENS,), jnp.int32).at[positions].set(jnp.arange(TOKENS, dtype=jnp.int32))
    pad_index = jnp.concatenate([jnp.zeros((3,), jnp.int32), inverse])
    seg_padded = jnp.concatenate([jnp.full((3,), -1, jnp.int32), segments.astype(jnp.int32)])
    step_size = jax.nn.softplus(step_raw + step_bias[:, None])
    log_decay = -decay_rate[:, None] * step_size

    def advance(carried, block_index):
        block_start = (block_index * BLOCK).astype(jnp.int32)
        row_index = lax.dynamic_slice_in_dim(pad_index, block_start, BLOCK + 3)
        seg_window = lax.dynamic_slice_in_dim(seg_padded, block_start, BLOCK + 3)
        live_rows = (seg_window >= 0)[:, None]

        def rows_of(source):
            return jnp.where(live_rows, source[row_index], jnp.zeros((), source.dtype))
        feature_conv = convolve(rows_of(inputs), conv_inputs, seg_window)
        write_conv = convolve(rows_of(writes), conv_writes, seg_window)
        read_conv = convolve(rows_of(reads), conv_reads, seg_window)
        body_index = row_index[3:]
        step_block = step_size[:, body_index].reshape(G, per_group, BLOCK)
        decay_block = log_decay[:, body_index].reshape(G, per_group, BLOCK)
        seg_block = seg_window[3:]
        seg_before = seg_window[2]
        features = feature_conv.reshape(BLOCK, G, per_group, P_SIZE)
        write_groups = write_conv.reshape(BLOCK, G, N)
        read_groups = read_conv.reshape(BLOCK, G, N)
        inner_part, state_add, block_decay, cumulative = block_parts(features, write_groups, read_groups, step_block, decay_block, seg_block, seg_before)
        inter_part = block_inter(read_groups, cumulative, seg_block, seg_before, carried)
        mixed = inner_part + inter_part + skip_gain.reshape(G, per_group)[None, :, :, None] * features.astype(jnp.float32)
        mixed = mixed.reshape(BLOCK, H * P_SIZE)
        gated_out = mixed * jax.nn.silu(gates[body_index].astype(jnp.float32))
        mean_square = lax.optimization_barrier(jnp.mean(gated_out * gated_out, axis=1, keepdims=True))
        normed = (gated_out * lax.rsqrt(mean_square + EPSILON) * norm_gain).astype(jnp.bfloat16)
        carried = block_decay[..., None, None] * carried + state_add
        return (carried, normed)
    start_state = jnp.zeros((G, per_group, P_SIZE, N), jnp.float32)
    _, blocks_out = lax.scan(advance, start_state, jnp.arange(TOKENS // BLOCK, dtype=jnp.int32))
    ordered = blocks_out.reshape(TOKENS, H * P_SIZE)
    return ordered[positions]
```

```python
import functools

import jax
import jax.numpy as jnp
from jax import lax
from jax.experimental import pallas as pl
from jax.experimental.pallas import tpu as pltpu
from jax.sharding import PartitionSpec as P

H = 128
P_SIZE = 128
N = 128
G = 8
Q = 256
EPSILON = 1e-05
LOG2E = 1.4426950408889634
MESH = pl.DeviceIdType.MESH
MIB = 2**20
F32 = jnp.float32
BF16 = jnp.bfloat16

TAIL, CUM, ENTER, ENTER_HALF, INFO = 0, 16, 32, 48, 64


def silu_of_half(h):
    return h + h * jnp.tanh(h)


def conv_tile(ext, taps, cols, masked):
    total = ext[8:] * taps[3:4]
    for back in (1, 2, 3):
        term = pltpu.roll(ext, back, 0)[8:] * taps[3 - back : 4 - back]
        if masked:
            term = term * cols[:, INFO + back : INFO + back + 1]
        total = total + term
    return silu_of_half(total)


def local_kernel(
    flags,
    x_ref, w_ref, r_ref, step_ref, bias_ref, rate_ref, info_ref, halo_ref, taps_ref,
    feat_ref, wc_ref, rc_ref, cols_ref, brow_ref, sloc_ref, msg_ref,
    state, prev, carry, upper,
):
    i = pl.program_id(0)
    per_half = pl.num_programs(0) // 2
    at = lax.rem(i, per_half)
    width = x_ref.shape[1]
    heads = step_ref.shape[0]

    @pl.when(i == 0)
    def _():
        row = lax.broadcasted_iota(jnp.int32, (Q, Q), 0)
        col = lax.broadcasted_iota(jnp.int32, (Q, Q), 1)
        upper[...] = jnp.where(row <= col, 1.0, 0.0).astype(F32)

    @pl.when(at == 0)
    def _():
        state[...] = jnp.zeros_like(state)
        carry[...] = jnp.zeros_like(carry)
        prev[...] = halo_ref[0]

    step = jax.nn.softplus(step_ref[...] + bias_ref[...])
    decay = step * rate_ref[...]
    cum = jnp.dot(decay, upper[...], precision=lax.Precision.HIGHEST, preferred_element_type=F32)
    info = info_ref[...]
    seg, before, before_half, seg_end = info[0:1], info[4:5], info[5:6], info[6:7]
    cum_end = cum[:, Q - 1 : Q]
    tail = jnp.where(seg == seg_end, jnp.exp2(cum_end - cum) * step, 0.0)
    enter = jnp.where(seg == before, jnp.exp2(cum), 0.0)
    base = carry[:, 0:1]
    enter_half = jnp.where(seg == before_half, jnp.exp2(base + cum), 0.0)
    block_decay = enter[:, Q - 1 : Q]
    half_decay = enter_half[:, Q - 1 : Q]
    carry[...] = jnp.broadcast_to(base + cum_end, carry.shape)
    brow_ref[...] = cum - jnp.log2(step)
    fill = jnp.zeros((128 - INFO - 8, Q), F32)
    cols_ref[...] = jnp.transpose(
        jnp.concatenate([tail, cum, enter, enter_half, info, fill], axis=0)
    )

    def work(masked):
        cols = cols_ref[...]

        def conv(block, c0, c1):
            cur = block.astype(F32)
            ext = jnp.concatenate([prev[:, c0:c1], cur], axis=0)
            prev[:, c0:c1] = cur[Q - 8 :]
            return conv_tile(ext, taps_ref[:, c0:c1], cols, masked)

        wc = conv(w_ref[...], width, width + N)
        rc = conv(r_ref[...], width + N, width + 2 * N)
        wc_ref[...] = wc.astype(BF16)
        rc_ref[...] = rc.astype(BF16)
        wct = jnp.transpose(wc).astype(BF16)
        for pair in range(heads // 2):
            scaled = []
            for h in (2 * pair, 2 * pair + 1):
                c0, c1 = h * P_SIZE, (h + 1) * P_SIZE
                feat = conv(x_ref[:, c0:c1], c0, c1).astype(BF16)
                feat_ref[:, c0:c1] = feat
                scaled.append((feat.astype(F32) * cols[:, TAIL + h : TAIL + h + 1]).astype(BF16))
            add = jnp.dot(wct, jnp.concatenate(scaled, axis=1), preferred_element_type=F32)
            for k in (0, 1):
                h = 2 * pair + k
                c0, c1 = h * P_SIZE, (h + 1) * P_SIZE
                old = state[:, c0:c1]
                sloc_ref[0, :, c0:c1] = old.astype(BF16)
                new = old * block_decay[h : h + 1] + add[:, k * P_SIZE : (k + 1) * P_SIZE]
                state[:, c0:c1] = new

    @pl.when(flags[1 + i] == 0)
    def _():
        work(False)

    @pl.when(flags[1 + i] != 0)
    def _():
        work(True)

    @pl.when(at == per_half - 1)
    def _():
        for h in range(heads):
            msg_ref[h, 0, :N] = state[:, h * P_SIZE : (h + 1) * P_SIZE].astype(BF16)
            whole = jnp.broadcast_to(half_decay[h : h + 1], (8, P_SIZE))
            high = whole.astype(BF16).astype(F32)
            msg_ref[h, 0, N:] = jnp.concatenate([high, whole - high], axis=0).astype(BF16)


def exchange_kernel(n, msg_ref, out_ref, recv, back, s1, r1, s2, r2):
    me = lax.axis_index("seq")
    barrier = pltpu.get_barrier_semaphore()
    for k in range(1, n):
        pl.semaphore_signal(barrier, inc=1, device_id={"seq": lax.rem(me + k, n)}, device_id_type=MESH)
    pl.semaphore_wait(barrier, n - 1)

    def trip(src, dst, send, arrive):
        copies = []
        for k in range(1, n):
            to = lax.rem(me + k, n)
            copy = pltpu.make_async_remote_copy(
                src_ref=src.at[to], dst_ref=dst.at[me], send_sem=send.at[k], recv_sem=arrive.at[k],
                device_id={"seq": to}, device_id_type=MESH,
            )
            copy.start()
            copies.append(copy)
        return copies

    copies = trip(msg_ref, recv, s1, r1)
    recv[me] = msg_ref[me]
    for copy in copies:
        copy.wait()

    def advance(total, src, half):
        back[src, half] = total.astype(BF16)
        decay = recv[src, half, N : N + 1].astype(F32) + recv[src, half, N + 8 : N + 9].astype(F32)
        return total * decay + recv[src, half, :N].astype(F32)

    total = jnp.zeros((N, P_SIZE), F32)
    for src in range(n):
        total = advance(total, src, 0)
    for src in range(n - 1, -1, -1):
        total = advance(total, src, 1)
    copies = trip(back, out_ref, s2, r2)
    out_ref[me] = back[me]
    for copy in copies:
        copy.wait()


def inner_kernel(
    feat_ref, wc_ref, rc_ref, cols_ref, brow_ref, info_ref, sloc_ref, skip_ref, y_ref
):
    heads = brow_ref.shape[0]
    cols = cols_ref[...]
    rc = rc_ref[...]
    scores = lax.dot_general(rc, wc_ref[...], (((1,), (1,)), ((), ())), preferred_element_type=F32)
    row = lax.broadcasted_iota(jnp.int32, (Q, Q), 0)
    col = lax.broadcasted_iota(jnp.int32, (Q, Q), 1)
    keep = (cols[:, INFO : INFO + 1] == info_ref[0:1]) & (col <= row)
    scores = jnp.where(keep, scores, 0.0)
    half = Q // 2
    for pair in range(heads // 2):
        inter = jnp.dot(
            rc, sloc_ref[0, :, pair * 2 * P_SIZE : (pair + 1) * 2 * P_SIZE], preferred_element_type=F32
        )
        for k in (0, 1):
            h = 2 * pair + k
            c0, c1 = h * P_SIZE, (h + 1) * P_SIZE
            feat = feat_ref[:, c0:c1]
            cum = jnp.broadcast_to(cols[:, CUM + h : CUM + h + 1], (Q, P_SIZE))
            brow = brow_ref[h : h + 1, :]

            def tile(t, s):
                spread = cum[t * half : (t + 1) * half] - brow[:, s * half : (s + 1) * half]
                part = scores[t * half : (t + 1) * half, s * half : (s + 1) * half]
                return (part * jnp.exp2(spread)).astype(BF16)

            top = jnp.dot(tile(0, 0), feat[:half], preferred_element_type=F32)
            low = jnp.dot(
                jnp.concatenate([tile(1, 0), tile(1, 1)], axis=1), feat, preferred_element_type=F32
            )
            y = jnp.concatenate([top, low], axis=0)
            y = y + inter[:, k * P_SIZE : (k + 1) * P_SIZE] * cols[:, ENTER + h : ENTER + h + 1]
            y = y + feat.astype(F32) * skip_ref[:, c0:c1]
            y_ref[:, c0:c1] = y.astype(BF16)


def gate_kernel(swapped, y_ref, gate_ref, rc_ref, cols_ref, sin_ref, out_ref, sq_ref):
    heads = sin_ref.shape[0]
    cols = cols_ref[...]
    rc = rc_ref[...]
    squares = jnp.zeros((Q, P_SIZE), F32)
    for pair in range(heads // 2):
        both = jnp.concatenate([sin_ref[2 * pair, 0], sin_ref[2 * pair + 1, 0]], axis=1)
        inter = jnp.dot(rc, both, preferred_element_type=F32)
        for k in (0, 1):
            h = 2 * pair + k
            c0, c1 = h * P_SIZE, (h + 1) * P_SIZE
            y = y_ref[:, c0:c1].astype(F32)
            y = y + inter[:, k * P_SIZE : (k + 1) * P_SIZE] * cols[:, ENTER_HALF + h : ENTER_HALF + h + 1]
            gated = y * silu_of_half(gate_ref[:, c0:c1].astype(F32) * 0.5)
            squares = squares + gated * gated
            out_ref[:, c0:c1] = gated.astype(BF16)
    sums = jnp.sum(jnp.transpose(squares), axis=0, keepdims=True)
    sq_ref[0] = jnp.concatenate([sums[:, :128], sums[:, 128:]], axis=0)


def sum_kernel(n, mine_ref, out_ref, recv, send, arrive):
    me = lax.axis_index("head")
    barrier = pltpu.get_barrier_semaphore()
    for k in range(1, n):
        pl.semaphore_signal(barrier, inc=1, device_id={"head": lax.rem(me + k, n)}, device_id_type=MESH)
    pl.semaphore_wait(barrier, n - 1)
    copies = []
    for k in range(1, n):
        copy = pltpu.make_async_remote_copy(
            src_ref=mine_ref, dst_ref=recv.at[k], send_sem=send.at[k], recv_sem=arrive.at[k],
            device_id={"head": lax.rem(me + k, n)}, device_id_type=MESH,
        )
        copy.start()
        copies.append(copy)
    total = mine_ref[...]
    for k in range(1, n):
        copies[k - 1].wait()
        total = total + recv[k]
    out_ref[...] = lax.rsqrt(total / (H * P_SIZE) + EPSILON)


def norm_kernel(gated_ref, scale_ref, gain_ref, out_ref):
    scale = scale_ref[0]
    row = jnp.concatenate([scale[0:1], scale[1:2]], axis=1)
    col = jnp.transpose(jnp.broadcast_to(row, (128, Q)))
    for c in range(gated_ref.shape[1] // 128):
        c0, c1 = c * 128, (c + 1) * 128
        out_ref[:, c0:c1] = (gated_ref[:, c0:c1].astype(F32) * col * gain_ref[:, c0:c1]).astype(BF16)


def on_device(
    inputs, gates, writes, reads, step_raw, step_bias, decay_rate, skip_gain,
    conv_inputs, conv_writes, conv_reads, norm_gain, positions, segments,
):
    tokens, width = inputs.shape
    heads = step_raw.shape[0]
    half_rows = tokens // 2
    chunks = tokens // Q
    per_half = chunks // 2
    n_seq, n_head = lax.axis_size("seq"), lax.axis_size("head")
    first_start, second_start = positions[0], positions[half_rows]
    swapped = first_start > second_start

    def tail_rows(end):
        parts = [a[end - 8 : end] for a in (inputs, writes, reads)]
        return jnp.concatenate(parts, axis=1)

    first_tail, second_tail = tail_rows(half_rows), tail_rows(tokens)
    low_tail = jnp.where(swapped, second_tail, first_tail)
    high_tail = jnp.where(swapped, first_tail, second_tail)
    ends = n_seq - 1
    prev_low = lax.ppermute(low_tail, "seq", [(i, i + 1) for i in range(ends)])
    prev_high = lax.ppermute(high_tail, "seq", [(i + 1, i) for i in range(ends)])
    prev_high = jnp.where(lax.axis_index("seq") == ends, low_tail, prev_high)
    halo = jnp.stack(
        [jnp.where(swapped, prev_high, prev_low), jnp.where(swapped, prev_low, prev_high)]
    ).astype(F32)

    seg_padded = jnp.concatenate([jnp.full((3,), -1, jnp.int32), segments])
    windows = jnp.stack(
        [lax.dynamic_slice_in_dim(seg_padded, s, half_rows + 3) for s in (first_start, second_start)]
    )
    seg = windows[:, 3:]
    same = [seg == windows[:, 3 - k : 3 - k + half_rows] for k in (1, 2, 3)]
    before = jnp.broadcast_to(windows[:, 2 : 2 + half_rows : Q, None], (2, per_half, Q))
    seg_end = jnp.broadcast_to(seg[:, Q - 1 :: Q, None], (2, per_half, Q))
    before_half = jnp.broadcast_to(windows[:, 2:3], (2, half_rows))
    info = jnp.stack(
        [a.reshape(tokens).astype(F32) for a in (seg, *same, before, before_half, seg_end, jnp.zeros_like(seg))]
    )
    broken = jnp.any(~same[2].reshape(chunks, Q), axis=1)
    flags = jnp.concatenate([swapped[None], broken]).astype(jnp.int32)
    taps = jnp.concatenate([conv_inputs, conv_writes, conv_reads], axis=1).astype(F32) * 0.5
    taps = jnp.concatenate([taps, jnp.zeros_like(taps)], axis=0)

    rows = lambda cols: pl.BlockSpec((Q, cols), lambda i, *_: (i, 0))
    lanes = lambda n: pl.BlockSpec((n, Q), lambda i, *_: (0, i))
    whole = lambda *shape: pl.BlockSpec(shape, lambda i, *_: (0,) * len(shape))
    params = pltpu.CompilerParams(vmem_limit_bytes=48 * MIB)
    wide = width + 2 * N
    message = N + 16

    feat, wc, rc, cols, brow, sloc, msg = pl.pallas_call(
        local_kernel,
        grid_spec=pltpu.PrefetchScalarGridSpec(
            num_scalar_prefetch=1,
            grid=(chunks,),
            in_specs=[
                rows(width), rows(N), rows(N), lanes(heads), whole(heads, 1), whole(heads, 1), lanes(8),
                pl.BlockSpec((1, 8, wide), lambda i, f: (i // per_half, 0, 0)), whole(8, wide),
            ],
            out_specs=[
                rows(width), rows(N), rows(N), rows(128), lanes(heads),
                pl.BlockSpec((1, N, width), lambda i, f: (i, 0, 0)),
                pl.BlockSpec((heads, 1, message, P_SIZE), lambda i, f: (0, (i // per_half) ^ f[0], 0, 0)),
            ],
            scratch_shapes=[
                pltpu.VMEM((N, width), F32), pltpu.VMEM((8, wide), F32),
                pltpu.VMEM((heads, 128), F32), pltpu.VMEM((Q, Q), F32),
            ],
        ),
        out_shape=[
            jax.ShapeDtypeStruct((tokens, width), BF16),
            jax.ShapeDtypeStruct((tokens, N), BF16),
            jax.ShapeDtypeStruct((tokens, N), BF16),
            jax.ShapeDtypeStruct((tokens, 128), F32),
            jax.ShapeDtypeStruct((heads, tokens), F32),
            jax.ShapeDtypeStruct((chunks, N, width), BF16),
            jax.ShapeDtypeStruct((heads, 2, message, P_SIZE), BF16),
        ],
        compiler_params=params,
        name="local",
    )(
        flags, inputs, writes, reads, step_raw, step_bias[:, None], -LOG2E * decay_rate[:, None],
        info, halo, taps,
    )

    vmem = pl.BlockSpec(memory_space=pltpu.VMEM)
    entering = pl.pallas_call(
        functools.partial(exchange_kernel, n_seq),
        in_specs=[vmem],
        out_specs=vmem,
        out_shape=jax.ShapeDtypeStruct((n_seq, 2, N, P_SIZE), BF16),
        scratch_shapes=[
            pltpu.VMEM((n_seq, 2, message, P_SIZE), BF16), pltpu.VMEM((n_seq, 2, N, P_SIZE), BF16),
        ] + [pltpu.SemaphoreType.DMA((n_seq,))] * 4,
        compiler_params=pltpu.CompilerParams(
            collective_id=0, has_side_effects=True, vmem_limit_bytes=32 * MIB
        ),
        name="exchange",
    )(msg)

    y = pl.pallas_call(
        inner_kernel,
        grid=(chunks,),
        in_specs=[
            rows(width), rows(N), rows(N), rows(128), lanes(heads), lanes(8),
            pl.BlockSpec((1, N, width), lambda i: (i, 0, 0)), whole(1, width),
        ],
        out_specs=rows(width),
        out_shape=jax.ShapeDtypeStruct((tokens, width), BF16),
        compiler_params=params,
        name="inner",
    )(feat, wc, rc, cols, brow, info, sloc, jnp.repeat(skip_gain, P_SIZE)[None])

    gated, squares = pl.pallas_call(
        gate_kernel,
        grid_spec=pltpu.PrefetchScalarGridSpec(
            num_scalar_prefetch=1,
            grid=(chunks,),
            in_specs=[
                rows(width), rows(width), rows(N), rows(128),
                pl.BlockSpec((heads, 1, N, P_SIZE), lambda i, f: (0, (i // per_half) ^ f[0], 0, 0)),
            ],
            out_specs=[rows(width), pl.BlockSpec((1, Q // 128, 128), lambda i, f: (i, 0, 0))],
        ),
        out_shape=[
            jax.ShapeDtypeStruct((tokens, width), BF16),
            jax.ShapeDtypeStruct((chunks, Q // 128, 128), F32),
        ],
        compiler_params=params,
        name="gate",
    )(flags, y, gates, rc, cols, entering)

    scale = pl.pallas_call(
        functools.partial(sum_kernel, n_head),
        in_specs=[vmem],
        out_specs=vmem,
        out_shape=jax.ShapeDtypeStruct(squares.shape, F32),
        scratch_shapes=[pltpu.VMEM((n_head, *squares.shape), F32)] + [pltpu.SemaphoreType.DMA((n_head,))] * 2,
        compiler_params=pltpu.CompilerParams(collective_id=1, has_side_effects=True),
        name="sum",
    )(squares)

    return pl.pallas_call(
        norm_kernel,
        grid=(chunks,),
        in_specs=[rows(width), pl.BlockSpec((1, Q // 128, 128), lambda i: (i, 0, 0)), whole(1, width)],
        out_specs=rows(width),
        out_shape=jax.ShapeDtypeStruct((tokens, width), BF16),
        compiler_params=params,
        name="norm",
    )(gated, scale, norm_gain[None])


def solution(mesh):
    return jax.shard_map(
        on_device,
        mesh=mesh,
        in_specs=(
            P("seq", "head"), P("seq", "head"), P("seq", "head"), P("seq", "head"), P("head", "seq"),
            P("head"), P("head"), P("head"), P(None, "head"), P(None, "head"), P(None, "head"),
            P("head"), P("seq"), P(),
        ),
        out_specs=P("seq", "head"),
        check_vma=False,
    )
```

```python
import functools

import jax
import jax.numpy as jnp
from jax import lax
from jax.experimental import pallas as pl
from jax.experimental.pallas import tpu as pltpu
from jax.sharding import PartitionSpec as P

H = 128
P_SIZE = 128
N = 128
G = 8
Q = 256
SETS = 2
EPSILON = 1e-05
LOG2E = 1.4426950408889634
MESH = pl.DeviceIdType.MESH
MIB = 2**20
F32 = jnp.float32
BF16 = jnp.bfloat16
MESSAGE = N + 16
RIM = 16


def silu_of_half(h):
    return h + h * jnp.tanh(h)


def conv_tile(ext, taps, masks):
    total = ext[8:] * taps[3:4]
    for back in (1, 2, 3):
        total = total + pltpu.roll(ext, back, 0)[8:] * taps[3 - back : 4 - back] * masks[back - 1]
    return silu_of_half(total)


def spread_out(cols, lane, width=P_SIZE):
    return jnp.broadcast_to(cols[:, lane : lane + 1], (cols.shape[0], width))


def head_order(n, sets):
    if n == 16 and sets == 2:
        return [0, 2, 5, 7, 8, 10, 13, 15, 1, 3, 4, 6, 9, 11, 12, 14]
    return list(range(n))


def main_kernel(
    n_seq, n_head, comm, phases,
    x_hbm, gate_hbm, write_ref, read_ref, step_ref, bias_ref, rate_ref, info_ref, flip_ref, taps_ref, skip_ref,
    out_hbm, scale_ref,
    body, gate, wct, wc, rc, cols, brow, decay, half_decay, sloc, state, prev, carry,
    upper, scores, squares, sq, rim_mine, rim_in, msg, recv, back, entering, sums,
    x_sem, g_sem, o_sem, t_sem, h_send, h_recv, s1, r1, s2, r2, s3, r3,
):
    tokens, width = body.shape
    heads = width // P_SIZE
    chunks = tokens // Q
    per_half = chunks // 2
    half_rows = tokens // 2
    per_set = heads // SETS
    set_width = per_set * P_SIZE
    me = lax.axis_index("seq") if comm else 0
    my_head = lax.axis_index("head") if comm else 0
    device_of = head_order(n_seq, SETS)
    TAIL, CUM, ENTER, ENTER_HALF, INFO = (k * per_set for k in range(5))

    def rows_of(c):
        return pl.ds(pl.multiple_of(c * Q, Q), Q)

    def x_copy(c):
        return pltpu.make_async_copy(x_hbm.at[rows_of(c)], body.at[rows_of(c)], x_sem.at[c])

    def gate_copy(c):
        return pltpu.make_async_copy(gate_hbm.at[rows_of(c)], gate.at[rows_of(c)], g_sem.at[c])

    def out_copy(c):
        return pltpu.make_async_copy(body.at[rows_of(c)], out_hbm.at[rows_of(c)], o_sem.at[c])

    def tail_copy(k):
        end = half_rows * (k + 1)
        return pltpu.make_async_copy(
            x_hbm.at[pl.ds(end - RIM, RIM)], rim_in.at[k, :, pl.ds(0, width)], t_sem.at[k]
        )

    for k in (0, 1):
        tail_copy(k).start()
    for c in range(chunks):
        x_copy(c).start()
    for c in range(chunks):
        gate_copy(c).start()

    if comm:
        barrier = pltpu.get_barrier_semaphore()
        for k in range(1, n_seq):
            pl.semaphore_signal(barrier, inc=1, device_id={"seq": lax.rem(me + k, n_seq)}, device_id_type=MESH)
        for k in range(1, n_head):
            pl.semaphore_signal(barrier, inc=1, device_id={"head": lax.rem(my_head + k, n_head)}, device_id_type=MESH)

    flip = flip_ref[0:1, 0:1]

    def pick(second, here, there):
        return jnp.where(jnp.broadcast_to(second, here.shape) > 0.5, there, here)

    for k in (0, 1):
        tail_copy(k).wait()
        end = half_rows * (k + 1)
        rim_in[k, :, width : width + N] = write_ref[end - RIM : end]
        rim_in[k, :, width + N :] = read_ref[end - RIM : end]
    first, second = rim_in[0].astype(F32), rim_in[1].astype(F32)
    rim_mine[0] = pick(flip, first, second).astype(BF16)
    rim_mine[1] = pick(flip, second, first).astype(BF16)
    rim_copies = []
    if comm:
        pl.semaphore_wait(barrier, n_seq - 1 + n_head - 1)
        for k, to in ((0, lax.rem(me + 1, n_seq)), (1, lax.rem(me + n_seq - 1, n_seq))):
            rim_copies.append(
                pltpu.make_async_remote_copy(
                    src_ref=rim_mine.at[k], dst_ref=rim_in.at[2 + k], send_sem=h_send.at[k],
                    recv_sem=h_recv.at[k], device_id={"seq": to}, device_id_type=MESH,
                )
            )
            rim_copies[-1].start()

    row = lax.broadcasted_iota(jnp.int32, (Q, Q), 0)
    col = lax.broadcasted_iota(jnp.int32, (Q, Q), 1)
    upper[...] = jnp.where(row <= col, 1.0, 0.0).astype(F32)
    state[...] = jnp.zeros_like(state)

    def prepare(c, _):
        at = pl.ds(pl.multiple_of(c * Q, Q), Q)
        step = jax.nn.softplus(step_ref[:, at] + bias_ref[...])
        cum = jnp.dot(
            step * rate_ref[...], upper[...], precision=lax.Precision.HIGHEST, preferred_element_type=F32
        )
        info = info_ref[:, at]
        seg, before, before_half, seg_end = info[0:1], info[4:5], info[5:6], info[6:7]
        cum_end = cum[:, Q - 1 : Q]
        base = jnp.where(lax.rem(c, per_half) == 0, 0.0, carry[:, 0:1])
        tail = jnp.where(seg == seg_end, jnp.exp2(cum_end - cum) * step, 0.0)
        enter = jnp.where(seg == before, jnp.exp2(cum), 0.0)
        enter_half = jnp.where(seg == before_half, jnp.exp2(base + cum), 0.0)
        decay[c] = jnp.broadcast_to(enter[:, Q - 1 : Q], (heads, 128))
        half_decay[c] = jnp.broadcast_to(enter_half[:, Q - 1 : Q], (heads, 128))
        carry[...] = jnp.broadcast_to(base + cum_end, carry.shape)
        brow[c] = cum - jnp.log2(step)
        for g in range(SETS):
            own = slice(g * per_set, (g + 1) * per_set)
            fill = jnp.zeros((128 - 4 * per_set - 8, Q), F32)
            cols[g, rows_of(c)] = jnp.transpose(
                jnp.concatenate([tail[own], cum[own], enter[own], enter_half[own], info, fill], axis=0)
            )
        return 0

    if phases >= 1:
        lax.fori_loop(0, chunks, prepare, 0)

    if comm:
        for copy in rim_copies:
            copy.wait()
    low_in = rim_in[2, RIM - 8 :].astype(F32)
    high_in = rim_in[3, RIM - 8 :].astype(F32)
    if comm:
        high_in = jnp.where(me == n_seq - 1, rim_mine[0, RIM - 8 :].astype(F32), high_in)
    rims = (pick(flip, low_in, high_in), pick(flip, high_in, low_in))
    prev[0] = rims[0]
    prev[1] = rims[1]

    def masks_of(c):
        both = cols[0, rows_of(c)]
        return [spread_out(both, INFO + k) for k in (1, 2, 3)]

    def group_part(c, _):
        masks = masks_of(c)
        half = c // per_half

        def conv(ref, c0):
            cur = ref[rows_of(c)].astype(F32)
            ext = jnp.concatenate([prev[half, :, c0 : c0 + N], cur], axis=0)
            prev[half, :, c0 : c0 + N] = cur[Q - 8 :]
            return conv_tile(ext, taps_ref[:, c0 : c0 + N], masks)

        w = conv(write_ref, width)
        r = conv(read_ref, width + N)
        rc[rows_of(c)] = r.astype(BF16)
        wc[rows_of(c)] = w.astype(BF16)
        wct[c] = jnp.transpose(w).astype(BF16)
        return 0

    if phases >= 2:
        lax.fori_loop(0, chunks, group_part, 0)

    def local_part(k, _):
        g, c = k // chunks, lax.rem(k, chunks)
        half = c // per_half
        masks = masks_of(c)
        own = cols[g, rows_of(c)]

        @pl.when(g == 0)
        def _():
            x_copy(c).wait()

        for pair in range(per_set // 2):
            scaled = []
            at = pl.ds(pl.multiple_of(g * set_width + pair * 2 * P_SIZE, 2 * P_SIZE), 2 * P_SIZE)
            for j in (0, 1):
                h = 2 * pair + j
                one = pl.ds(pl.multiple_of(g * set_width + h * P_SIZE, P_SIZE), P_SIZE)
                cur = body[rows_of(c), one].astype(F32)
                ext = jnp.concatenate([prev[half, :, one], cur], axis=0)
                prev[half, :, one] = cur[Q - 8 :]
                feat = conv_tile(ext, taps_ref[:, one], masks).astype(BF16)
                body[rows_of(c), one] = feat
                scaled.append((feat.astype(F32) * spread_out(own, TAIL + h)).astype(BF16))
            add = jnp.dot(wct[c], jnp.concatenate(scaled, axis=1), preferred_element_type=F32)
            old = state[half, :, at]
            sloc[c, :, at] = old.astype(BF16)
            drow = [decay[c, pl.ds(g * per_set + 2 * pair + j, 1), :] for j in (0, 1)]
            state[half, :, at] = old * jnp.concatenate(drow, axis=1) + add
        return 0

    def send_states(g):
        for h in range(g * per_set, (g + 1) * per_set):
            at = slice(h * P_SIZE, (h + 1) * P_SIZE)
            first, second = state[0, :, at], state[1, :, at]
            msg[h, 0, :N] = pick(flip, first, second).astype(BF16)
            msg[h, 1, :N] = pick(flip, second, first).astype(BF16)
            dec = [jnp.broadcast_to(half_decay[k, h : h + 1], (8, 128)) for k in (per_half - 1, chunks - 1)]
            for k, whole in ((0, pick(flip, dec[0], dec[1])), (1, pick(flip, dec[1], dec[0]))):
                high = whole.astype(BF16).astype(F32)
                msg[h, k, N:] = jnp.concatenate([high, whole - high], axis=0).astype(BF16)
        if comm:
            for h in range(g * per_set, (g + 1) * per_set):
                to = device_of[h]

                @pl.when(me != to)
                def _():
                    state_copy(h).start()

                @pl.when(me == to)
                def _():
                    recv[me] = msg[h]

    def state_copy(h):
        return pltpu.make_async_remote_copy(
            src_ref=msg.at[h], dst_ref=recv.at[me], send_sem=s1.at[h], recv_sem=r1.at[me],
            device_id={"seq": device_of[h]}, device_id_type=MESH,
        )

    def state_arrival(src):
        return pltpu.make_async_remote_copy(
            src_ref=msg.at[0], dst_ref=recv.at[src], send_sem=s1.at[0], recv_sem=r1.at[src],
            device_id={"seq": src}, device_id_type=MESH,
        )

    def enter_copy(h, to):
        return pltpu.make_async_remote_copy(
            src_ref=back.at[to], dst_ref=entering.at[h], send_sem=s2.at[to], recv_sem=r2.at[h],
            device_id={"seq": to}, device_id_type=MESH,
        )

    def scan_states(g):
        if not comm:
            return
        for h in range(g * per_set, (g + 1) * per_set):
            @pl.when(me == device_of[h])
            def _():
                for src in range(n_seq):
                    @pl.when(me != src)
                    def _():
                        state_arrival(src).wait_recv()

                def advance(total, src, half):
                    back[src, half] = total.astype(BF16)
                    keep = recv[src, half, N : N + 1].astype(F32) + recv[src, half, N + 8 : N + 9].astype(F32)
                    return total * keep + recv[src, half, :N].astype(F32)

                total = lax.fori_loop(
                    0, n_seq, lambda k, t: advance(t, k, 0), jnp.zeros((N, P_SIZE), F32)
                )
                lax.fori_loop(0, n_seq, lambda k, t: advance(t, n_seq - 1 - k, 1), total)
                for to in range(n_seq):
                    if to != device_of[h]:
                        enter_copy(h, to).start()
                entering[h] = back[device_of[h]]

    if phases >= 3:
        for g in range(SETS):
            lax.fori_loop(g * chunks, (g + 1) * chunks, local_part, 0)
            send_states(g)

    def inner_part(k, _):
        g, c = k // chunks, lax.rem(k, chunks)
        own = cols[g, rows_of(c)]
        half = Q // 2

        @pl.when(g == 0)
        def _():
            gate_copy(c).wait()
            full = lax.dot_general(
                rc[rows_of(c)], wc[rows_of(c)], (((1,), (1,)), ((), ())), preferred_element_type=F32
            )
            seg_row = info_ref[0:1, pl.ds(pl.multiple_of(c * Q, Q), Q)]
            keep = (own[:, INFO : INFO + 1] == seg_row) & (col <= row)
            scores[c] = jnp.where(keep, full, 0.0)

        masked = scores[c]
        r = rc[rows_of(c)]
        for pair in range(per_set // 2):
            at = pl.ds(pl.multiple_of(g * set_width + pair * 2 * P_SIZE, 2 * P_SIZE), 2 * P_SIZE)
            inter = jnp.dot(r, sloc[c, :, at], preferred_element_type=F32)
            for j in (0, 1):
                h = 2 * pair + j
                one = pl.ds(pl.multiple_of(g * set_width + h * P_SIZE, P_SIZE), P_SIZE)
                feat = body[rows_of(c), one]
                cum = spread_out(own, CUM + h)
                bro = brow[c, pl.ds(g * per_set + h, 1), :]

                def tile(t, s):
                    spread = cum[t * half : (t + 1) * half] - bro[:, s * half : (s + 1) * half]
                    part = masked[t * half : (t + 1) * half, s * half : (s + 1) * half]
                    return (part * jnp.exp2(spread)).astype(BF16)

                top = jnp.dot(tile(0, 0), feat[:half], preferred_element_type=F32)
                low = jnp.dot(
                    jnp.concatenate([tile(1, 0), tile(1, 1)], axis=1), feat, preferred_element_type=F32
                )
                y = jnp.concatenate([top, low], axis=0)
                y = y + inter[:, j * P_SIZE : (j + 1) * P_SIZE] * spread_out(own, ENTER + h)
                y = y + feat.astype(F32) * skip_ref[:, one]
                sg = silu_of_half(gate[rows_of(c), one].astype(F32) * 0.5)
                gate[rows_of(c), one] = sg.astype(BF16)
                body[rows_of(c), one] = (y * sg).astype(BF16)
        return 0

    total_steps = SETS * chunks
    if phases >= 4:
        lax.fori_loop(0, 3, inner_part, 0)
        scan_states(0)
        lax.fori_loop(3, 12, inner_part, 0)
        scan_states(1)
        lax.fori_loop(12, total_steps, inner_part, 0)

    def finish_part(k, _):
        g, c = k // chunks, lax.rem(k, chunks)
        own = cols[g, rows_of(c)]
        r = rc[rows_of(c)]
        second = c >= per_half
        pick_high = jnp.where(second, 1.0 - flip, flip)
        total = jnp.where(g == 0, 0.0, squares[c])
        for pair in range(per_set // 2):
            states = []
            for j in (0, 1):
                h = g * per_set + 2 * pair + j
                low, high = entering[h, 0].astype(F32), entering[h, 1].astype(F32)
                states.append(pick(pick_high, low, high).astype(BF16))
            inter = jnp.dot(r, jnp.concatenate(states, axis=1), preferred_element_type=F32)
            for j in (0, 1):
                h = 2 * pair + j
                one = pl.ds(pl.multiple_of(g * set_width + h * P_SIZE, P_SIZE), P_SIZE)
                scaled = inter[:, j * P_SIZE : (j + 1) * P_SIZE] * spread_out(own, ENTER_HALF + h)
                gated = body[rows_of(c), one].astype(F32) + scaled * gate[rows_of(c), one].astype(F32)
                total = total + gated * gated
                body[rows_of(c), one] = gated.astype(BF16)
        squares[c] = total

        @pl.when(g == SETS - 1)
        def _():
            out_copy(c).start()
            sums_here = jnp.sum(jnp.transpose(total), axis=0, keepdims=True)
            sq[c] = jnp.concatenate([sums_here[:, :128], sums_here[:, 128:]], axis=0)

        return 0

    for g in range(SETS):
        if comm:
            for h in range(g * per_set, (g + 1) * per_set):
                @pl.when(me != device_of[h])
                def _():
                    enter_copy(h, device_of[h]).wait_recv()

        if phases >= 5:
            lax.fori_loop(g * chunks, (g + 1) * chunks, finish_part, 0)

    total = sq[...]
    if comm:
        copies = []
        for k in range(1, n_head):
            copies.append(
                pltpu.make_async_remote_copy(
                    src_ref=sq, dst_ref=sums.at[k], send_sem=s3.at[k], recv_sem=r3.at[k],
                    device_id={"head": lax.rem(my_head + k, n_head)}, device_id_type=MESH,
                )
            )
            copies[-1].start()
        for k in range(1, n_head):
            copies[k - 1].wait()
            total = total + sums[k]
        for h in range(heads):
            @pl.when(me != device_of[h])
            def _():
                state_copy(h).wait_send()
        for h in range(heads):
            @pl.when(me == device_of[h])
            def _():
                for to in range(n_seq):
                    if to != device_of[h]:
                        enter_copy(h, to).wait_send()
    scale_ref[...] = lax.rsqrt(total / (H * P_SIZE) + EPSILON)
    if phases >= 5:
        for c in range(chunks):
            out_copy(c).wait()
    if phases < 4:
        for c in range(chunks):
            gate_copy(c).wait()
    if phases < 3:
        for c in range(chunks):
            x_copy(c).wait()


def main_call(n_seq, n_head, comm, phases, inputs, gates, small):
    tokens, width = inputs.shape
    heads = width // P_SIZE
    chunks = tokens // Q
    wide = width + 2 * N
    vmem = pl.BlockSpec(memory_space=pltpu.VMEM)
    hbm = pl.BlockSpec(memory_space=pl.ANY)
    dma = lambda n: pltpu.SemaphoreType.DMA((n,))
    return pl.pallas_call(
        functools.partial(main_kernel, n_seq, n_head, comm, phases),
        in_specs=[hbm, hbm] + [vmem] * len(small),
        out_specs=[hbm, vmem],
        out_shape=[
            jax.ShapeDtypeStruct((tokens, width), BF16),
            jax.ShapeDtypeStruct((chunks, Q // 128, 128), F32),
        ],
        scratch_shapes=[
            pltpu.VMEM((tokens, width), BF16),
            pltpu.VMEM((tokens, width), BF16),
            pltpu.VMEM((chunks, N, Q), BF16),
            pltpu.VMEM((tokens, N), BF16),
            pltpu.VMEM((tokens, N), BF16),
            pltpu.VMEM((SETS, tokens, 128), F32),
            pltpu.VMEM((chunks, heads, Q), F32),
            pltpu.VMEM((chunks, heads, 128), F32),
            pltpu.VMEM((chunks, heads, 128), F32),
            pltpu.VMEM((chunks, N, width), BF16),
            pltpu.VMEM((2, N, width), F32),
            pltpu.VMEM((2, 8, wide), F32),
            pltpu.VMEM((heads, 128), F32),
            pltpu.VMEM((Q, Q), F32),
            pltpu.VMEM((chunks, Q, Q), F32),
            pltpu.VMEM((chunks, Q, P_SIZE), F32),
            pltpu.VMEM((chunks, Q // 128, 128), F32),
            pltpu.VMEM((2, RIM, wide), BF16),
            pltpu.VMEM((4, RIM, wide), BF16),
            pltpu.VMEM((heads, 2, MESSAGE, P_SIZE), BF16),
            pltpu.VMEM((n_seq, 2, MESSAGE, P_SIZE), BF16),
            pltpu.VMEM((n_seq, 2, N, P_SIZE), BF16),
            pltpu.VMEM((heads, 2, N, P_SIZE), BF16),
            pltpu.VMEM((n_head, chunks, Q // 128, 128), F32),
            dma(chunks), dma(chunks), dma(chunks), dma(2), dma(2), dma(2),
            dma(heads), dma(n_seq), dma(n_seq), dma(heads), dma(n_head), dma(n_head),
        ],
        compiler_params=pltpu.CompilerParams(
            vmem_limit_bytes=56 * MIB,
            **(dict(collective_id=0, has_side_effects=True) if comm else {}),
        ),
        name="main",
    )(inputs, gates, *small)


def norm_kernel(gated_ref, scale_ref, gain_ref, out_ref):
    for k in range(scale_ref.shape[0]):
        scale = scale_ref[k]
        row = jnp.concatenate([scale[0:1], scale[1:2]], axis=1)
        col = jnp.transpose(jnp.broadcast_to(row, (128, Q)))
        at = slice(k * Q, (k + 1) * Q)
        for c in range(gated_ref.shape[1] // 128):
            c0, c1 = c * 128, (c + 1) * 128
            out_ref[at, c0:c1] = (gated_ref[at, c0:c1].astype(F32) * col * gain_ref[:, c0:c1]).astype(BF16)


def norm_call(gated, scale, gain):
    tokens, width = gated.shape
    block = 2 * Q
    rows = pl.BlockSpec((block, width), lambda i: (i, 0))
    return pl.pallas_call(
        norm_kernel,
        grid=(tokens // block,),
        in_specs=[
            rows, pl.BlockSpec((block // Q, Q // 128, 128), lambda i: (i, 0, 0)),
            pl.BlockSpec((1, width), lambda i: (0, 0)),
        ],
        out_specs=rows,
        out_shape=jax.ShapeDtypeStruct((tokens, width), BF16),
        compiler_params=pltpu.CompilerParams(vmem_limit_bytes=32 * MIB),
        name="norm",
    )(gated, scale, gain)


def on_device(
    inputs, gates, writes, reads, step_raw, step_bias, decay_rate, skip_gain,
    conv_inputs, conv_writes, conv_reads, norm_gain, positions, segments,
    comm=True, phases=5,
):
    tokens, width = inputs.shape
    half_rows = tokens // 2
    chunks = tokens // Q
    per_half = chunks // 2
    n_seq = lax.axis_size("seq") if comm else 16
    n_head = lax.axis_size("head") if comm else 8
    first_start, second_start = positions[0], positions[half_rows]
    swapped = first_start > second_start

    seg_padded = jnp.concatenate([jnp.full((3,), -1, jnp.int32), segments])
    windows = jnp.stack(
        [lax.dynamic_slice_in_dim(seg_padded, s, half_rows + 3) for s in (first_start, second_start)]
    )
    seg = windows[:, 3:]
    same = [seg == windows[:, 3 - k : 3 - k + half_rows] for k in (1, 2, 3)]
    before = jnp.broadcast_to(windows[:, 2 : 2 + half_rows : Q, None], (2, per_half, Q))
    seg_end = jnp.broadcast_to(seg[:, Q - 1 :: Q, None], (2, per_half, Q))
    before_half = jnp.broadcast_to(windows[:, 2:3], (2, half_rows))
    info = jnp.stack(
        [a.reshape(tokens).astype(F32) for a in (seg, *same, before, before_half, seg_end, jnp.zeros_like(seg))]
    )
    flip = jnp.broadcast_to(swapped.astype(F32), (8, 128))
    taps = jnp.concatenate([conv_inputs, conv_writes, conv_reads], axis=1).astype(F32) * 0.5
    small = (
        writes, reads, step_raw, step_bias[:, None], -LOG2E * decay_rate[:, None], info, flip, taps,
        jnp.repeat(skip_gain, P_SIZE)[None],
    )
    gated, scale = main_call(n_seq, n_head, comm, phases, inputs, gates, small)
    return norm_call(gated, scale, norm_gain[None])


def solution(mesh):
    return jax.shard_map(
        on_device,
        mesh=mesh,
        in_specs=(
            P("seq", "head"), P("seq", "head"), P("seq", "head"), P("seq", "head"), P("head", "seq"),
            P("head"), P("head"), P("head"), P(None, "head"), P(None, "head"), P(None, "head"),
            P("head"), P("seq"), P(),
        ),
        out_specs=P("seq", "head"),
        check_vma=False,
    )
```

```python
import functools

import jax
import jax.numpy as jnp
from jax import lax
from jax.experimental import pallas as pl
from jax.experimental.pallas import tpu as pltpu
from jax.sharding import PartitionSpec as P

H = 128
P_SIZE = 128
N = 128
G = 8
Q = 256
SETS = 2
SCAN_AT = (4, 12)
VMEM_MAIN = 52
EPSILON = 1e-05
LOG2E = 1.4426950408889634
MESH = pl.DeviceIdType.MESH
MIB = 2**20
F32 = jnp.float32
BF16 = jnp.bfloat16
MESSAGE = N + 16
RIM = 16


def silu_of_half(h):
    return h + h * jnp.tanh(h)


def spread_out(cols, lane, width=P_SIZE):
    return jnp.broadcast_to(cols[:, lane : lane + 1], (cols.shape[0], width))


def scan_device(h, n):
    side = 4 if n == 16 else 1
    per_set = n // SETS
    g, j = h // per_set, h % per_set
    per_row = per_set // side
    y = j // per_row
    return y * (n // side) + (j % per_row) * SETS + (g - y) % SETS


def scan_head(me, n):
    side = 4 if n == 16 else 1
    per_row = n // SETS // side
    y, z = me // (n // side), lax.rem(me, n // side)
    g = lax.rem(y + z, SETS)
    return g, g * (n // SETS) + y * per_row + z // SETS


def main_kernel(
    n_seq, n_head, comm, phases,
    x_hbm, gate_hbm, write_ref, read_ref, step_ref, bias_ref, rate_ref, skip_ref, ci_ref, cw_ref, cr_ref,
    seg_ref, pos_ref,
    out_hbm, scale_ref,
    raw, feats, gate, wct, r_enter, r_half, cols, frow, trow, segs, decay, half_decay, loc_scale, half_scale,
    sloc, state, raw_group, taps, skips, shifts, upper, scores, squares, sq, rim_own, rim_mine, rim_in,
    msg, recv, back, entering, sums,
    x_sem, g_sem, o_sem, t_sem, h_send, h_recv, s1, r1, s2, r2, s3, r3,
):
    tokens, width = feats.shape
    heads = width // P_SIZE
    chunks = tokens // Q
    per_half = chunks // 2
    half_rows = tokens // 2
    per_set = heads // SETS
    set_width = per_set * P_SIZE
    side = Q // 2
    me = lax.axis_index("seq") if comm else 0
    my_head = lax.axis_index("head") if comm else 0
    my_set, my_scan = scan_head(me, n_seq)
    device_of = [scan_device(h, n_seq) for h in range(heads)]
    CUM, INFO = 0, heads
    first, second = pos_ref[0], pos_ref[half_rows]
    flip = jnp.where(first > second, 1, 0)

    def rows_of(c):
        return pl.ds(pl.multiple_of(c * Q, Q), Q)

    def lanes_of(start, count):
        return pl.ds(pl.multiple_of(start, P_SIZE), count)

    def window_of(c, rim):
        start = c * Q + (c // per_half) * RIM
        return pl.ds(pl.multiple_of(start if rim else start + RIM, RIM), Q + RIM if rim else Q)

    def x_copy(c):
        return pltpu.make_async_copy(x_hbm.at[rows_of(c)], raw.at[window_of(c, False)], x_sem.at[c])

    def gate_copy(c):
        return pltpu.make_async_copy(gate_hbm.at[rows_of(c)], gate.at[rows_of(c)], g_sem.at[c])

    def out_copy(c):
        return pltpu.make_async_copy(feats.at[rows_of(c)], out_hbm.at[rows_of(c)], o_sem.at[c])

    def tail_copy(k):
        end = half_rows * (k + 1)
        return pltpu.make_async_copy(
            x_hbm.at[pl.ds(end - RIM, RIM)], rim_own.at[k, :, pl.ds(0, width)], t_sem.at[k]
        )

    for k in (0, 1):
        tail_copy(k).start()
    for c in range(chunks):
        x_copy(c).start()
    for c in range(chunks):
        gate_copy(c).start()

    if comm:
        barrier = pltpu.get_barrier_semaphore()
        for k in range(1, n_seq):
            pl.semaphore_signal(barrier, inc=1, device_id={"seq": lax.rem(me + k, n_seq)}, device_id_type=MESH)
        for k in range(1, n_head):
            pl.semaphore_signal(barrier, inc=1, device_id={"head": lax.rem(my_head + k, n_head)}, device_id_type=MESH)

    for k in (0, 1):
        tail_copy(k).wait()
        end = half_rows * (k + 1)
        rim_own[k, :, width : width + N] = write_ref[end - RIM : end]
        rim_own[k, :, width + N :] = read_ref[end - RIM : end]
    rim_mine[0] = rim_own[flip]
    rim_mine[1] = rim_own[1 - flip]
    rim_copies = []
    if comm:
        pl.semaphore_wait(barrier, n_seq - 1 + n_head - 1)
        for k, to in ((0, lax.rem(me + 1, n_seq)), (1, lax.rem(me + n_seq - 1, n_seq))):
            rim_copies.append(
                pltpu.make_async_remote_copy(
                    src_ref=rim_mine.at[k], dst_ref=rim_in.at[k], send_sem=h_send.at[k],
                    recv_sem=h_recv.at[k], device_id={"seq": to}, device_id_type=MESH,
                )
            )
            rim_copies[-1].start()

    taps[:, :width] = ci_ref[...].astype(F32) * 0.5
    taps[:, width : width + N] = cw_ref[...].astype(F32) * 0.5
    taps[:, width + N :] = cr_ref[...].astype(F32) * 0.5
    state[...] = jnp.zeros_like(state)
    eye = lax.broadcasted_iota(jnp.int32, (heads, heads), 0) == lax.broadcasted_iota(jnp.int32, (heads, heads), 1)

    def column(ref):
        return jnp.sum(jnp.where(eye, jnp.broadcast_to(ref[...], (heads, heads)), 0.0), axis=1, keepdims=True)

    bias, rate = column(bias_ref), column(rate_ref) * -LOG2E
    skips[...] = jnp.broadcast_to(column(skip_ref), (heads, P_SIZE))
    lane = lax.broadcasted_iota(jnp.int32, (1, half_rows), 1)
    for k, start in ((0, first), (1, second)):
        at = start // half_rows

        def in_a_row(block):
            return jnp.concatenate([block[j : j + 1] for j in range(half_rows // 128)], axis=1).astype(F32)

        here = in_a_row(seg_ref[at])
        ahead = in_a_row(seg_ref[jnp.maximum(at - 1, 0)])
        ahead = jnp.where(jnp.full(ahead.shape, at, jnp.int32) > 0, ahead, -1.0)
        lines = [here]
        for ago in (1, 2, 3):
            lines.append(jnp.where(lane < ago, pltpu.roll(ahead, ago, 1), pltpu.roll(here, ago, 1)))
        for j, line in enumerate(lines):
            segs[j : j + 1, k * half_rows : (k + 1) * half_rows] = line

    row = lax.broadcasted_iota(jnp.int32, (Q, Q), 0)
    col = lax.broadcasted_iota(jnp.int32, (Q, Q), 1)
    upper[...] = jnp.where(row <= col, 1.0, 0.0).astype(F32)

    def by_chunk(one_of):
        return jnp.concatenate([one_of(c) for c in range(chunks)], axis=0)

    def chunk_lanes(c):
        return slice(c * Q, (c + 1) * Q)

    def prepare():
        raw_step = by_chunk(lambda c: step_ref[:, chunk_lanes(c)])
        step = jax.nn.softplus(raw_step + by_chunk(lambda c: bias))
        cum = jnp.dot(
            step * by_chunk(lambda c: rate), upper[...], precision=lax.Precision.HIGHEST, preferred_element_type=F32
        )
        cum_end = cum[:, Q - 1 : Q]
        middle = 0.5 * cum_end
        grown = jnp.exp2(cum - middle)
        factor = jnp.exp2(middle - cum) * step
        tail = jnp.exp2(cum_end - cum) * step
        wide = (heads, 128)
        for c in range(chunks):
            own = slice(c * heads, (c + 1) * heads)
            at = chunk_lanes(c)
            seg, one_ago = segs[0:1, at], segs[1:2, at]
            half_start = (c // per_half) * half_rows
            same = [jnp.where(seg == segs[k : k + 1, at], 1.0, 0.0) for k in (1, 2, 3)]
            enters = jnp.where(seg == one_ago[:, 0:1], 1.0, 0.0)
            enters_half = jnp.where(seg == segs[1:2, half_start : half_start + 1], 1.0, 0.0)
            leaves = jnp.where(seg == seg[:, Q - 1 : Q], 1.0, 0.0)
            base = jnp.zeros((heads, 1), F32) if c % per_half == 0 else base + end
            end, mid = cum_end[own], middle[own]
            frow[c] = factor[own]
            trow[c] = tail[own] * leaves
            decay[c] = jnp.broadcast_to(jnp.exp2(end) * enters[:, Q - 1 : Q], wide)
            half_decay[c] = jnp.broadcast_to(jnp.exp2(base + end) * enters_half[:, Q - 1 : Q], wide)
            loc_scale[c] = jnp.broadcast_to(jnp.exp2(mid), wide)
            half_scale[c] = jnp.broadcast_to(jnp.exp2(base + mid), wide)
            fill = jnp.zeros((128 - heads - 6, Q), F32)
            cols[c * Q : (c + 1) * Q] = jnp.transpose(
                jnp.concatenate([grown[own], seg, *same, enters, enters_half, fill], axis=0)
            )

    if phases >= 1:
        prepare()

    if comm:
        for copy in rim_copies:
            copy.wait()
        rim_in[1] = jnp.where(
            jnp.full(rim_in.shape[1:], me) == n_seq - 1, rim_mine[0].astype(F32), rim_in[1].astype(F32)
        ).astype(BF16)
    for k, rim in ((0, rim_in[flip]), (1, rim_in[1 - flip])):
        start = k * (half_rows + RIM)
        raw[start : start + RIM] = rim[:, :width]
        raw_group[start : start + RIM] = rim[:, width:]
        for j, ref in ((0, write_ref), (1, read_ref)):
            raw_group[start + RIM : start + RIM + half_rows, j * N : (j + 1) * N] = ref[
                k * half_rows : (k + 1) * half_rows
            ]

    to_row = lax.broadcasted_iota(jnp.int32, (side, RIM + side), 0)
    from_row = lax.broadcasted_iota(jnp.int32, (side, RIM + side), 1)

    def conv(source, c, lanes, tap_lanes):
        tap = [taps[k : k + 1, tap_lanes] for k in range(4)]
        x = source[window_of(c, True), lanes]
        out = []
        for b in (0, 1):
            moved = jnp.dot(shifts[2 * c + b], x[b * side : RIM + (b + 1) * side], preferred_element_type=F32)
            total = x[RIM + b * side : RIM + (b + 1) * side].astype(F32) * tap[3]
            for k in (1, 2, 3):
                total = total + moved[(k - 1) * side : k * side] * tap[3 - k]
            out.append(silu_of_half(total))
        return jnp.concatenate(out, axis=0)

    def group_part(c, _):
        info = cols[rows_of(c)]
        for b in (0, 1):
            for k in (1, 2, 3):
                same = spread_out(info[b * side : (b + 1) * side], INFO + k, RIM + side)
                hit = jnp.where(from_row == to_row + (RIM - k), same, 0.0)
                shifts[2 * c + b, (k - 1) * side : k * side] = hit.astype(BF16)
        both = conv(raw_group, c, slice(0, 2 * N), slice(width, width + 2 * N))
        w, r = both[:, :N], both[:, N:]
        wct[c] = jnp.transpose(w.astype(BF16).astype(F32))
        w, r = w.astype(BF16), r.astype(BF16)
        wide = r.astype(F32)
        r_enter[rows_of(c)] = (wide * spread_out(info, INFO + 4)).astype(BF16)
        r_half[rows_of(c)] = (wide * spread_out(info, INFO + 5)).astype(BF16)
        full = lax.dot_general(r, w, (((1,), (1,)), ((), ())), preferred_element_type=F32)
        seg_row = segs[0:1, lanes_of(c * Q, Q)]
        keep = (info[:, INFO : INFO + 1] == seg_row) & (col <= row)
        scores[c] = jnp.where(keep, full, 0.0)
        return 0

    if phases >= 2:
        lax.fori_loop(0, chunks, group_part, 0)

    def conv_part(g, c, _):
        if g == 0:
            x_copy(c).wait()
        for pair in range(per_set // 2):
            start = g * set_width + pair * 2 * P_SIZE
            at = slice(start, start + 2 * P_SIZE)
            feats[rows_of(c), at] = conv(raw, c, at, at).astype(BF16)
        return 0

    def state_part(g, c, _):
        half = c // per_half
        w = wct[c]
        for h in range(g * per_set, (g + 1) * per_set):
            one = slice(h, h + 1)
            scaled = (w * trow[c, one, :]).astype(BF16)
            add = jnp.dot(scaled, feats[rows_of(c), h * P_SIZE : (h + 1) * P_SIZE], preferred_element_type=F32)
            old = state[half, h]
            sloc[c, h] = (old * loc_scale[c, one, :]).astype(BF16)
            state[half, h] = old * decay[c, one, :] + add
        return 0

    def state_copy(h):
        return pltpu.make_async_remote_copy(
            src_ref=msg.at[h], dst_ref=recv.at[me], send_sem=s1.at[h], recv_sem=r1.at[me],
            device_id={"seq": device_of[h]}, device_id_type=MESH,
        )

    def state_arrival(src):
        return pltpu.make_async_remote_copy(
            src_ref=msg.at[0], dst_ref=recv.at[src], send_sem=s1.at[0], recv_sem=r1.at[src],
            device_id={"seq": src}, device_id_type=MESH,
        )

    def enter_copy(g, h, to):
        return pltpu.make_async_remote_copy(
            src_ref=back.at[to], dst_ref=entering[g].at[h - g * per_set], send_sem=s2.at[to], recv_sem=r2.at[h],
            device_id={"seq": to}, device_id_type=MESH,
        )

    def send_states(g):
        for h in range(g * per_set, (g + 1) * per_set):
            for k, half in ((0, flip), (1, 1 - flip)):
                msg[h, k, :N] = state[half, h].astype(BF16)
                whole = jnp.broadcast_to(half_decay[(half + 1) * per_half - 1, h : h + 1], (8, 128))
                high = whole.astype(BF16).astype(F32)
                msg[h, k, N:] = jnp.concatenate([high, whole - high], axis=0).astype(BF16)
            if comm:
                to = device_of[h]

                @pl.when(me != to)
                def _():
                    state_copy(h).start()

                @pl.when(me == to)
                def _():
                    recv[me] = msg[h]

    def scan_states(g):
        if not comm:
            return

        @pl.when(my_set == g)
        def _():
            for k in range(1, n_seq):
                state_arrival(lax.rem(me + k, n_seq)).wait_recv()

            def advance(total, src, half):
                back[src, half] = total.astype(BF16)
                keep = recv[src, half, N : N + 1].astype(F32) + recv[src, half, N + 8 : N + 9].astype(F32)
                return total * keep + recv[src, half, :N].astype(F32)

            total = lax.fori_loop(0, n_seq, lambda k, t: advance(t, k, 0), jnp.zeros((N, P_SIZE), F32))
            lax.fori_loop(0, n_seq, lambda k, t: advance(t, n_seq - 1 - k, 1), total)
            for k in range(1, n_seq):
                enter_copy(g, my_scan, lax.rem(me + k, n_seq)).start()
            entering[g][my_scan - g * per_set] = back[me]

    if phases >= 3:
        for g in range(SETS):
            lax.fori_loop(0, chunks, functools.partial(conv_part, g), 0)
            lax.fori_loop(0, chunks, functools.partial(state_part, g), 0)
            send_states(g)

    def inner_part(g, c, _):
        info = cols[rows_of(c)]
        if g == 0:
            gate_copy(c).wait()

        masked = scores[c]
        r = r_enter[rows_of(c)]
        for j in range(per_set):
            h = g * per_set + j
            one = slice(h * P_SIZE, (h + 1) * P_SIZE)
            feat = feats[rows_of(c), one]
            fac = frow[c, h : h + 1, :]
            top = jnp.concatenate([r[:side], (masked[:side, :side] * fac[:, :side]).astype(BF16)], axis=1)
            low = jnp.concatenate([r[side:], (masked[side:] * fac).astype(BF16)], axis=1)
            entry = sloc[c, h]
            y = jnp.concatenate(
                [
                    jnp.dot(top, jnp.concatenate([entry, feat[:side]], axis=0), preferred_element_type=F32),
                    jnp.dot(low, jnp.concatenate([entry, feat], axis=0), preferred_element_type=F32),
                ],
                axis=0,
            )
            grown = spread_out(info, CUM + h)
            opened = silu_of_half(gate[rows_of(c), one].astype(F32) * 0.5)
            y = (y * grown + feat.astype(F32) * skips[h : h + 1, :]) * opened
            gate[rows_of(c), one] = (grown * opened).astype(BF16)
            raw[rows_of(c), one] = y.astype(BF16)
        return 0

    def inner_steps(start, stop):
        for g in range(SETS):
            begin, end = max(start - g * chunks, 0), min(stop - g * chunks, chunks)
            if begin < end:
                lax.fori_loop(begin, end, functools.partial(inner_part, g), 0)

    if phases >= 4:
        done = 0
        for g, until in enumerate(SCAN_AT):
            inner_steps(done, until)
            scan_states(g)
            done = until
        inner_steps(done, SETS * chunks)

    def finish_part(g, c, _):
        r = r_half[rows_of(c)]
        which = jnp.where(c >= per_half, 1 - flip, flip)
        total = jnp.zeros((Q, P_SIZE), F32) if g == 0 else squares[c]
        for pair in range(per_set // 2):
            states = []
            for j in (0, 1):
                h = g * per_set + 2 * pair + j
                states.append((entering[g][2 * pair + j, which].astype(F32) * half_scale[c, h : h + 1, :]).astype(BF16))
            inter = jnp.dot(r, jnp.concatenate(states, axis=1), preferred_element_type=F32)
            for j in (0, 1):
                start = g * set_width + (2 * pair + j) * P_SIZE
                one = slice(start, start + P_SIZE)
                gated = raw[rows_of(c), one].astype(F32)
                gated = gated + inter[:, j * P_SIZE : (j + 1) * P_SIZE] * gate[rows_of(c), one].astype(F32)
                total = total + gated * gated
                feats[rows_of(c), one] = gated.astype(BF16)
        if g < SETS - 1:
            squares[c] = total
        else:
            out_copy(c).start()
            sums_here = jnp.sum(jnp.transpose(total), axis=0, keepdims=True)
            sq[c] = jnp.concatenate([sums_here[:, :128], sums_here[:, 128:]], axis=0)

        return 0

    for g in range(SETS):
        if comm:
            for h in range(g * per_set, (g + 1) * per_set):
                @pl.when(me != device_of[h])
                def _():
                    enter_copy(g, h, device_of[h]).wait_recv()

        if phases >= 5:
            lax.fori_loop(0, chunks, functools.partial(finish_part, g), 0)

    total = sq[...]
    if comm:
        copies = []
        for k in range(1, n_head):
            copies.append(
                pltpu.make_async_remote_copy(
                    src_ref=sq, dst_ref=sums.at[k], send_sem=s3.at[k], recv_sem=r3.at[k],
                    device_id={"head": lax.rem(my_head + k, n_head)}, device_id_type=MESH,
                )
            )
            copies[-1].start()
        for h in range(heads):
            @pl.when(me != device_of[h])
            def _():
                state_copy(h).wait_send()
        for k in range(1, n_seq):
            enter_copy(0, 0, lax.rem(me + k, n_seq)).wait_send()
        for k in range(1, n_head):
            copies[k - 1].wait()
            total = total + sums[k]
    scale_ref[...] = lax.rsqrt(total / (H * P_SIZE) + EPSILON)
    if phases >= 5:
        for c in range(chunks):
            out_copy(c).wait()
    if phases < 4:
        for c in range(chunks):
            gate_copy(c).wait()
    if phases < 3:
        for c in range(chunks):
            x_copy(c).wait()


def main_call(n_seq, n_head, comm, phases, inputs, gates, small, positions):
    tokens, width = inputs.shape
    heads = width // P_SIZE
    chunks = tokens // Q
    wide = width + 2 * N
    vmem = pl.BlockSpec(memory_space=pltpu.VMEM)
    hbm = pl.BlockSpec(memory_space=pl.ANY)
    dma = lambda n: pltpu.SemaphoreType.DMA((n,))
    return pl.pallas_call(
        functools.partial(main_kernel, n_seq, n_head, comm, phases),
        in_specs=[hbm, hbm] + [vmem] * len(small) + [pl.BlockSpec(memory_space=pltpu.SMEM)],
        out_specs=[hbm, vmem],
        out_shape=[
            jax.ShapeDtypeStruct((tokens, width), BF16),
            jax.ShapeDtypeStruct((chunks, Q // 128, 128), F32),
        ],
        scratch_shapes=[
            pltpu.VMEM((tokens + 2 * RIM, width), BF16),
            pltpu.VMEM((tokens, width), BF16),
            pltpu.VMEM((tokens, width), BF16),
            pltpu.VMEM((chunks, N, Q), F32),
            pltpu.VMEM((tokens, N), BF16),
            pltpu.VMEM((tokens, N), BF16),
            pltpu.VMEM((tokens, 128), F32),
            pltpu.VMEM((chunks, heads, Q), F32),
            pltpu.VMEM((chunks, heads, Q), F32),
            pltpu.VMEM((8, tokens), F32),
            pltpu.VMEM((chunks, heads, 128), F32),
            pltpu.VMEM((chunks, heads, 128), F32),
            pltpu.VMEM((chunks, heads, 128), F32),
            pltpu.VMEM((chunks, heads, 128), F32),
            pltpu.VMEM((chunks, heads, N, P_SIZE), BF16),
            pltpu.VMEM((2, heads, N, P_SIZE), F32),
            pltpu.VMEM((tokens + 2 * RIM, 2 * N), BF16),
            pltpu.VMEM((4, wide), F32),
            pltpu.VMEM((heads, P_SIZE), F32),
            pltpu.VMEM((2 * chunks, 3 * Q // 2, RIM + Q // 2), BF16),
            pltpu.VMEM((Q, Q), F32),
            pltpu.VMEM((chunks, Q, Q), F32),
            pltpu.VMEM((chunks, Q, P_SIZE), F32),
            pltpu.VMEM((chunks, Q // 128, 128), F32),
            pltpu.VMEM((2, RIM, wide), BF16),
            pltpu.VMEM((2, RIM, wide), BF16),
            pltpu.VMEM((2, RIM, wide), BF16),
            pltpu.VMEM((heads, 2, MESSAGE, P_SIZE), BF16),
            pltpu.VMEM((n_seq, 2, MESSAGE, P_SIZE), BF16),
            pltpu.VMEM((n_seq, 2, N, P_SIZE), BF16),
            (pltpu.VMEM((heads // SETS, 2, N, P_SIZE), BF16),) * SETS,
            pltpu.VMEM((n_head, chunks, Q // 128, 128), F32),
            dma(chunks), dma(chunks), dma(chunks), dma(2), dma(2), dma(2),
            dma(heads), dma(n_seq), dma(n_seq), dma(heads), dma(n_head), dma(n_head),
        ],
        compiler_params=pltpu.CompilerParams(
            vmem_limit_bytes=VMEM_MAIN * MIB,
            **(dict(collective_id=0, has_side_effects=True) if comm else {}),
        ),
        name="main",
    )(inputs, gates, *small, positions)


def norm_kernel(gated_ref, scale_ref, gain_ref, out_ref):
    for k in range(scale_ref.shape[0]):
        scale = scale_ref[k]
        row = jnp.concatenate([scale[0:1], scale[1:2]], axis=1)
        col = jnp.transpose(jnp.broadcast_to(row, (128, Q)))
        at = slice(k * Q, (k + 1) * Q)
        for c in range(gated_ref.shape[1] // 128):
            c0, c1 = c * 128, (c + 1) * 128
            out_ref[at, c0:c1] = (gated_ref[at, c0:c1].astype(F32) * col * gain_ref[:, c0:c1]).astype(BF16)


def norm_call(gated, scale, gain):
    tokens, width = gated.shape
    block = 2 * Q
    rows = pl.BlockSpec((block, width), lambda i: (i, 0))
    return pl.pallas_call(
        norm_kernel,
        grid=(tokens // block,),
        in_specs=[
            rows, pl.BlockSpec((block // Q, Q // 128, 128), lambda i: (i, 0, 0)),
            pl.BlockSpec((1, width), lambda i: (0, 0)),
        ],
        out_specs=rows,
        out_shape=jax.ShapeDtypeStruct((tokens, width), BF16),
        compiler_params=pltpu.CompilerParams(vmem_limit_bytes=60 * MIB),
        name="norm",
    )(gated, scale, gain)


def on_device(
    inputs, gates, writes, reads, step_raw, step_bias, decay_rate, skip_gain,
    conv_inputs, conv_writes, conv_reads, norm_gain, positions, segments,
    comm=True, phases=5,
):
    tokens, width = inputs.shape
    half_rows = tokens // 2
    n_seq = lax.axis_size("seq") if comm else 16
    n_head = lax.axis_size("head") if comm else 8
    small = (
        writes, reads, step_raw, step_bias[None], decay_rate[None], skip_gain[None],
        conv_inputs, conv_writes, conv_reads, segments.reshape(-1, half_rows // 128, 128),
    )
    gated, scale = main_call(n_seq, n_head, comm, phases, inputs, gates, small, positions)
    return norm_call(gated, scale, norm_gain[None])


def solution(mesh):
    return jax.shard_map(
        on_device,
        mesh=mesh,
        in_specs=(
            P("seq", "head"), P("seq", "head"), P("seq", "head"), P("seq", "head"), P("head", "seq"),
            P("head"), P("head"), P("head"), P(None, "head"), P(None, "head"), P(None, "head"),
            P("head"), P("seq"), P(),
        ),
        out_specs=P("seq", "head"),
        check_vma=False,
    )
```

```python
import functools

import jax
import jax.numpy as jnp
from jax import lax
from jax.experimental import pallas as pl
from jax.experimental.pallas import tpu as pltpu
from jax.sharding import PartitionSpec as P

H = 128
P_SIZE = 128
N = 128
G = 8
Q = 256
SETS = 4
VMEM_MAIN = 60
SCAN_AFTER_SENDING = ((), (), (0,), ())
SCAN_AFTER_INNER = {0: (1,), 1: (2,), 4: (3,)}
EPSILON = 1e-05
LOG2E = 1.4426950408889634
MESH = pl.DeviceIdType.MESH
MIB = 2**20
F32 = jnp.float32
BF16 = jnp.bfloat16
MESSAGE = N + 16
RIM = 16


def silu_of_half(h):
    return h + h * jnp.tanh(h)


def spread_out(cols, lane, width=P_SIZE):
    return jnp.broadcast_to(cols[:, lane : lane + 1], (cols.shape[0], width))


def scan_device(h, n):
    side = 4 if n == 16 else 1
    per_set = n // SETS
    g, j = h // per_set, h % per_set
    per_row = per_set // side
    y = j // per_row
    return y * (n // side) + (j % per_row) * SETS + (g - y) % SETS


def scan_head(me, n):
    side = 4 if n == 16 else 1
    per_row = n // SETS // side
    y, z = me // (n // side), lax.rem(me, n // side)
    g = lax.rem(y + z, SETS)
    return g, g * (n // SETS) + y * per_row + z // SETS


def main_kernel(
    n_seq, n_head, comm, phases,
    x_hbm, gate_hbm, write_ref, read_ref, step_ref, bias_ref, rate_ref, skip_ref, ci_ref, cw_ref, cr_ref,
    seg_ref, pos_ref,
    out_hbm, scale_ref,
    raw, feats, gate, wct, wc, r_enter, r_half, cols, frow, trow, segs, decay, half_decay, loc_scale, half_scale,
    sloc, state, raw_group, taps, skips, shifts, upper, scores, sq, rim_own, rim_mine, rim_in,
    msg, recv, back, entering, sums,
    x_sem, g_sem, o_sem, t_sem, h_send, h_recv, s1, r1, s2, r2, s3, r3,
):
    tokens, width = feats.shape
    heads = width // P_SIZE
    chunks = tokens // Q
    per_half = chunks // 2
    half_rows = tokens // 2
    per_set = heads // SETS
    set_width = per_set * P_SIZE
    side = Q // 2
    me = lax.axis_index("seq") if comm else 0
    my_head = lax.axis_index("head") if comm else 0
    my_set, my_scan = scan_head(me, n_seq)
    device_of = [scan_device(h, n_seq) for h in range(heads)]
    CUM, INFO = 0, heads
    first, second = pos_ref[0], pos_ref[half_rows]
    flip = jnp.where(first > second, 1, 0)

    def rows_of(c):
        return pl.ds(pl.multiple_of(c * Q, Q), Q)

    def lanes_of(start, count):
        return pl.ds(pl.multiple_of(start, P_SIZE), count)

    def window_of(c, rim):
        start = c * Q + (c // per_half) * RIM
        return pl.ds(pl.multiple_of(start if rim else start + RIM, RIM), Q + RIM if rim else Q)

    def x_copy(c):
        return pltpu.make_async_copy(x_hbm.at[rows_of(c)], raw.at[window_of(c, False)], x_sem.at[c])

    def gate_copy(c):
        return pltpu.make_async_copy(gate_hbm.at[rows_of(c)], gate.at[rows_of(c)], g_sem.at[c])

    def out_copy(c):
        return pltpu.make_async_copy(feats.at[rows_of(c)], out_hbm.at[rows_of(c)], o_sem.at[c])

    def tail_copy(k):
        end = half_rows * (k + 1)
        return pltpu.make_async_copy(
            x_hbm.at[pl.ds(end - RIM, RIM)], rim_own.at[k, :, pl.ds(0, width)], t_sem.at[k]
        )

    for k in (0, 1):
        tail_copy(k).start()
    for c in range(chunks):
        x_copy(c).start()
    for c in range(chunks):
        gate_copy(c).start()

    if comm:
        barrier = pltpu.get_barrier_semaphore()
        for k in range(1, n_seq):
            pl.semaphore_signal(barrier, inc=1, device_id={"seq": lax.rem(me + k, n_seq)}, device_id_type=MESH)
        for k in range(1, n_head):
            pl.semaphore_signal(barrier, inc=1, device_id={"head": lax.rem(my_head + k, n_head)}, device_id_type=MESH)

    for k in (0, 1):
        tail_copy(k).wait()
        end = half_rows * (k + 1)
        rim_own[k, :, width : width + N] = write_ref[end - RIM : end]
        rim_own[k, :, width + N :] = read_ref[end - RIM : end]
    rim_mine[0] = rim_own[flip]
    rim_mine[1] = rim_own[1 - flip]
    rim_copies = []
    if comm:
        pl.semaphore_wait(barrier, n_seq - 1 + n_head - 1)
        for k, to in ((0, lax.rem(me + 1, n_seq)), (1, lax.rem(me + n_seq - 1, n_seq))):
            rim_copies.append(
                pltpu.make_async_remote_copy(
                    src_ref=rim_mine.at[k], dst_ref=rim_in.at[k], send_sem=h_send.at[k],
                    recv_sem=h_recv.at[k], device_id={"seq": to}, device_id_type=MESH,
                )
            )
            rim_copies[-1].start()

    taps[:, :width] = ci_ref[...].astype(F32) * 0.5
    taps[:, width : width + N] = cw_ref[...].astype(F32) * 0.5
    taps[:, width + N :] = cr_ref[...].astype(F32) * 0.5
    state[...] = jnp.zeros_like(state)
    eye = lax.broadcasted_iota(jnp.int32, (heads, heads), 0) == lax.broadcasted_iota(jnp.int32, (heads, heads), 1)

    def column(ref):
        return jnp.sum(jnp.where(eye, jnp.broadcast_to(ref[...], (heads, heads)), 0.0), axis=1, keepdims=True)

    bias, rate = column(bias_ref), column(rate_ref) * -LOG2E
    skips[...] = jnp.broadcast_to(column(skip_ref), (heads, P_SIZE))
    lane = lax.broadcasted_iota(jnp.int32, (1, half_rows), 1)
    for k, start in ((0, first), (1, second)):
        at = start // half_rows

        def in_a_row(block):
            return jnp.concatenate([block[j : j + 1] for j in range(half_rows // 128)], axis=1).astype(F32)

        here = in_a_row(seg_ref[at])
        ahead = in_a_row(seg_ref[jnp.maximum(at - 1, 0)])
        ahead = jnp.where(jnp.full(ahead.shape, at, jnp.int32) > 0, ahead, -1.0)
        lines = [here]
        for ago in (1, 2, 3):
            lines.append(jnp.where(lane < ago, pltpu.roll(ahead, ago, 1), pltpu.roll(here, ago, 1)))
        for j, line in enumerate(lines):
            segs[j : j + 1, k * half_rows : (k + 1) * half_rows] = line

    row = lax.broadcasted_iota(jnp.int32, (Q, Q), 0)
    col = lax.broadcasted_iota(jnp.int32, (Q, Q), 1)
    upper[...] = jnp.where(row <= col, 1.0, 0.0).astype(F32)

    def by_chunk(one_of):
        return jnp.concatenate([one_of(c) for c in range(chunks)], axis=0)

    def chunk_lanes(c):
        return slice(c * Q, (c + 1) * Q)

    def prepare():
        raw_step = by_chunk(lambda c: step_ref[:, chunk_lanes(c)])
        step = jax.nn.softplus(raw_step + by_chunk(lambda c: bias))
        cum = jnp.dot(
            step * by_chunk(lambda c: rate), upper[...], precision=lax.Precision.HIGHEST, preferred_element_type=F32
        )
        cum_end = cum[:, Q - 1 : Q]
        middle = 0.5 * cum_end
        grown = jnp.exp2(cum - middle)
        factor = jnp.exp2(middle - cum) * step
        tail = jnp.exp2(cum_end - cum) * step
        wide = (heads, 128)
        for c in range(chunks):
            own = slice(c * heads, (c + 1) * heads)
            at = chunk_lanes(c)
            seg, one_ago = segs[0:1, at], segs[1:2, at]
            half_start = (c // per_half) * half_rows
            same = [jnp.where(seg == segs[k : k + 1, at], 1.0, 0.0) for k in (1, 2, 3)]
            enters = jnp.where(seg == one_ago[:, 0:1], 1.0, 0.0)
            enters_half = jnp.where(seg == segs[1:2, half_start : half_start + 1], 1.0, 0.0)
            leaves = jnp.where(seg == seg[:, Q - 1 : Q], 1.0, 0.0)
            base = jnp.zeros((heads, 1), F32) if c % per_half == 0 else base + end
            end, mid = cum_end[own], middle[own]
            frow[c] = factor[own]
            trow[c] = tail[own] * leaves
            decay[c] = jnp.broadcast_to(jnp.exp2(end) * enters[:, Q - 1 : Q], wide)
            half_decay[c] = jnp.broadcast_to(jnp.exp2(base + end) * enters_half[:, Q - 1 : Q], wide)
            loc_scale[c] = jnp.broadcast_to(jnp.exp2(mid), wide)
            half_scale[c] = jnp.broadcast_to(jnp.exp2(base + mid), wide)
            fill = jnp.zeros((128 - heads - 6, Q), F32)
            cols[c * Q : (c + 1) * Q] = jnp.transpose(
                jnp.concatenate([grown[own], seg, *same, enters, enters_half, fill], axis=0)
            )

    if phases >= 1:
        prepare()

    if comm:
        for copy in rim_copies:
            copy.wait()
        rim_in[1] = jnp.where(
            jnp.full(rim_in.shape[1:], me) == n_seq - 1, rim_mine[0].astype(F32), rim_in[1].astype(F32)
        ).astype(BF16)
    for k, rim in ((0, rim_in[flip]), (1, rim_in[1 - flip])):
        start = k * (half_rows + RIM)
        raw[start : start + RIM] = rim[:, :width]
        raw_group[start : start + RIM] = rim[:, width:]
        for j, ref in ((0, write_ref), (1, read_ref)):
            raw_group[start + RIM : start + RIM + half_rows, j * N : (j + 1) * N] = ref[
                k * half_rows : (k + 1) * half_rows
            ]

    to_row = lax.broadcasted_iota(jnp.int32, (side, RIM + side), 0)
    from_row = lax.broadcasted_iota(jnp.int32, (side, RIM + side), 1)

    def conv(source, c, lanes, tap_lanes):
        tap = [taps[k : k + 1, tap_lanes] for k in range(4)]
        x = source[window_of(c, True), lanes]
        out = []
        for b in (0, 1):
            moved = jnp.dot(shifts[2 * c + b], x[b * side : RIM + (b + 1) * side], preferred_element_type=F32)
            total = x[RIM + b * side : RIM + (b + 1) * side].astype(F32) * tap[3]
            for k in (1, 2, 3):
                total = total + moved[(k - 1) * side : k * side] * tap[3 - k]
            out.append(silu_of_half(total))
        return jnp.concatenate(out, axis=0)

    def write_part(c, _):
        info = cols[rows_of(c)]
        for b in (0, 1):
            for k in (1, 2, 3):
                same = spread_out(info[b * side : (b + 1) * side], INFO + k, RIM + side)
                hit = jnp.where(from_row == to_row + (RIM - k), same, 0.0)
                shifts[2 * c + b, (k - 1) * side : k * side] = hit.astype(BF16)
        w = conv(raw_group, c, slice(0, N), slice(width, width + N)).astype(BF16)
        wc[rows_of(c)] = w
        wct[c] = jnp.transpose(w.astype(F32))
        return 0

    if phases >= 2:
        lax.fori_loop(0, chunks, write_part, 0, unroll=2)

    def read_part(c, _):
        info = cols[rows_of(c)]
        r = conv(raw_group, c, slice(N, 2 * N), slice(width + N, width + 2 * N)).astype(BF16)
        wide = r.astype(F32)
        r_enter[rows_of(c)] = (wide * spread_out(info, INFO + 4)).astype(BF16)
        r_half[rows_of(c)] = (wide * spread_out(info, INFO + 5)).astype(BF16)
        full = lax.dot_general(r, wc[rows_of(c)], (((1,), (1,)), ((), ())), preferred_element_type=F32)
        seg_row = segs[0:1, lanes_of(c * Q, Q)]
        keep = (info[:, INFO : INFO + 1] == seg_row) & (col <= row)
        scores[c] = jnp.where(keep, full, 0.0)
        return 0

    def conv_part(g, c, _):
        if g == 0:
            x_copy(c).wait()
        for pair in range(per_set // 2):
            start = g * set_width + pair * 2 * P_SIZE
            at = slice(start, start + 2 * P_SIZE)
            feats[rows_of(c), at] = conv(raw, c, at, at).astype(BF16)
        return 0

    def state_part(g, c, _):
        half = c // per_half
        w = wct[c]
        for h in range(g * per_set, (g + 1) * per_set):
            one = slice(h, h + 1)
            scaled = (w * trow[c, one, :]).astype(BF16)
            add = jnp.dot(scaled, feats[rows_of(c), h * P_SIZE : (h + 1) * P_SIZE], preferred_element_type=F32)
            old = state[half, h]
            sloc[c, h] = (old * loc_scale[c, one, :]).astype(BF16)
            state[half, h] = old * decay[c, one, :] + add
        return 0

    def state_copy(h):
        return pltpu.make_async_remote_copy(
            src_ref=msg.at[h], dst_ref=recv.at[me], send_sem=s1.at[h], recv_sem=r1.at[me],
            device_id={"seq": device_of[h]}, device_id_type=MESH,
        )

    def state_arrival(src):
        return pltpu.make_async_remote_copy(
            src_ref=msg.at[0], dst_ref=recv.at[src], send_sem=s1.at[0], recv_sem=r1.at[src],
            device_id={"seq": src}, device_id_type=MESH,
        )

    def enter_copy(g, h, to):
        return pltpu.make_async_remote_copy(
            src_ref=back.at[to], dst_ref=entering[g].at[h - g * per_set], send_sem=s2.at[to], recv_sem=r2.at[h],
            device_id={"seq": to}, device_id_type=MESH,
        )

    def send_states(g):
        for h in range(g * per_set, (g + 1) * per_set):
            for k, half in ((0, flip), (1, 1 - flip)):
                msg[h, k, :N] = state[half, h].astype(BF16)
                whole = jnp.broadcast_to(half_decay[(half + 1) * per_half - 1, h : h + 1], (8, 128))
                high = whole.astype(BF16).astype(F32)
                msg[h, k, N:] = jnp.concatenate([high, whole - high], axis=0).astype(BF16)
            if comm:
                to = device_of[h]

                @pl.when(me != to)
                def _():
                    state_copy(h).start()

                @pl.when(me == to)
                def _():
                    recv[me] = msg[h]

    def scan_states(g):
        if not comm:
            return

        @pl.when(my_set == g)
        def _():
            for k in range(1, n_seq):
                state_arrival(lax.rem(me + k, n_seq)).wait_recv()

            def advance(total, src, half):
                back[src, half] = total.astype(BF16)
                keep = recv[src, half, N : N + 1].astype(F32) + recv[src, half, N + 8 : N + 9].astype(F32)
                return total * keep + recv[src, half, :N].astype(F32)

            total = lax.fori_loop(0, n_seq, lambda k, t: advance(t, k, 0), jnp.zeros((N, P_SIZE), F32))
            lax.fori_loop(0, n_seq, lambda k, t: advance(t, n_seq - 1 - k, 1), total)
            for k in range(1, n_seq):
                enter_copy(g, my_scan, lax.rem(me + k, n_seq)).start()
            entering[g][my_scan - g * per_set] = back[me]

    if phases >= 3:
        for g in range(SETS):
            lax.fori_loop(0, chunks, functools.partial(conv_part, g), 0, unroll=2)
            lax.fori_loop(0, chunks, functools.partial(state_part, g), 0, unroll=4)
            send_states(g)
            for scanned in SCAN_AFTER_SENDING[g]:
                scan_states(scanned)

    def inner_part(c, _):
        info = cols[rows_of(c)]
        gate_copy(c).wait()

        masked = scores[c]
        r = r_enter[rows_of(c)]
        for h in range(heads):
            one = slice(h * P_SIZE, (h + 1) * P_SIZE)
            feat = feats[rows_of(c), one]
            fac = frow[c, h : h + 1, :]
            top = jnp.concatenate([r[:side], (masked[:side, :side] * fac[:, :side]).astype(BF16)], axis=1)
            low = jnp.concatenate([r[side:], (masked[side:] * fac).astype(BF16)], axis=1)
            entry = sloc[c, h]
            y = jnp.concatenate(
                [
                    jnp.dot(top, jnp.concatenate([entry, feat[:side]], axis=0), preferred_element_type=F32),
                    jnp.dot(low, jnp.concatenate([entry, feat], axis=0), preferred_element_type=F32),
                ],
                axis=0,
            )
            grown = spread_out(info, CUM + h)
            opened = silu_of_half(gate[rows_of(c), one].astype(F32) * 0.5)
            y = (y * grown + feat.astype(F32) * skips[h : h + 1, :]) * opened
            gate[rows_of(c), one] = (grown * opened).astype(BF16)
            raw[rows_of(c), one] = y.astype(BF16)
        return 0

    if phases >= 4:
        lax.fori_loop(0, chunks, read_part, 0, unroll=2)
        done = 0
        for until, scanned in [*SCAN_AFTER_INNER.items(), (chunks, ())]:
            lax.fori_loop(done, until, inner_part, 0)
            done = until
            for g in scanned:
                scan_states(g)

    def finish_part(c, _):
        r = r_half[rows_of(c)]
        which = jnp.where(c >= per_half, 1 - flip, flip)
        total = jnp.zeros((Q, P_SIZE), F32)
        for pair in range(heads // 2):
            states = []
            for h in (2 * pair, 2 * pair + 1):
                state_in = entering[h // per_set][h % per_set, which].astype(F32)
                states.append((state_in * half_scale[c, h : h + 1, :]).astype(BF16))
            inter = jnp.dot(r, jnp.concatenate(states, axis=1), preferred_element_type=F32)
            for j in (0, 1):
                start = (2 * pair + j) * P_SIZE
                one = slice(start, start + P_SIZE)
                gated = raw[rows_of(c), one].astype(F32)
                gated = gated + inter[:, j * P_SIZE : (j + 1) * P_SIZE] * gate[rows_of(c), one].astype(F32)
                total = total + gated * gated
                feats[rows_of(c), one] = gated.astype(BF16)
        out_copy(c).start()
        sums_here = jnp.sum(jnp.transpose(total), axis=0, keepdims=True)
        sq[c] = jnp.concatenate([sums_here[:, :128], sums_here[:, 128:]], axis=0)
        return 0

    if comm:
        for h in range(heads):
            @pl.when(me != device_of[h])
            def _():
                enter_copy(h // per_set, h, device_of[h]).wait_recv()

    if phases >= 5:
        lax.fori_loop(0, chunks, finish_part, 0)

    total = sq[...]
    if comm:
        copies = []
        for k in range(1, n_head):
            copies.append(
                pltpu.make_async_remote_copy(
                    src_ref=sq, dst_ref=sums.at[k], send_sem=s3.at[k], recv_sem=r3.at[k],
                    device_id={"head": lax.rem(my_head + k, n_head)}, device_id_type=MESH,
                )
            )
            copies[-1].start()
        for h in range(heads):
            @pl.when(me != device_of[h])
            def _():
                state_copy(h).wait_send()
        for k in range(1, n_seq):
            enter_copy(0, 0, lax.rem(me + k, n_seq)).wait_send()
        for k in range(1, n_head):
            copies[k - 1].wait()
            total = total + sums[k]
    scale_ref[...] = lax.rsqrt(total / (H * P_SIZE) + EPSILON)
    if phases >= 5:
        for c in range(chunks):
            out_copy(c).wait()
    if phases < 4:
        for c in range(chunks):
            gate_copy(c).wait()
    if phases < 3:
        for c in range(chunks):
            x_copy(c).wait()


def main_call(n_seq, n_head, comm, phases, inputs, gates, small, positions):
    tokens, width = inputs.shape
    heads = width // P_SIZE
    chunks = tokens // Q
    wide = width + 2 * N
    vmem = pl.BlockSpec(memory_space=pltpu.VMEM)
    hbm = pl.BlockSpec(memory_space=pl.ANY)
    dma = lambda n: pltpu.SemaphoreType.DMA((n,))
    return pl.pallas_call(
        functools.partial(main_kernel, n_seq, n_head, comm, phases),
        in_specs=[hbm, hbm] + [vmem] * len(small) + [pl.BlockSpec(memory_space=pltpu.SMEM)],
        out_specs=[hbm, vmem],
        out_shape=[
            jax.ShapeDtypeStruct((tokens, width), BF16),
            jax.ShapeDtypeStruct((chunks, Q // 128, 128), F32),
        ],
        scratch_shapes=[
            pltpu.VMEM((tokens + 2 * RIM, width), BF16),
            pltpu.VMEM((tokens, width), BF16),
            pltpu.VMEM((tokens, width), BF16),
            pltpu.VMEM((chunks, N, Q), F32),
            pltpu.VMEM((tokens, N), BF16),
            pltpu.VMEM((tokens, N), BF16),
            pltpu.VMEM((tokens, N), BF16),
            pltpu.VMEM((tokens, 128), F32),
            pltpu.VMEM((chunks, heads, Q), F32),
            pltpu.VMEM((chunks, heads, Q), F32),
            pltpu.VMEM((8, tokens), F32),
            pltpu.VMEM((chunks, heads, 128), F32),
            pltpu.VMEM((chunks, heads, 128), F32),
            pltpu.VMEM((chunks, heads, 128), F32),
            pltpu.VMEM((chunks, heads, 128), F32),
            pltpu.VMEM((chunks, heads, N, P_SIZE), BF16),
            pltpu.VMEM((2, heads, N, P_SIZE), F32),
            pltpu.VMEM((tokens + 2 * RIM, 2 * N), BF16),
            pltpu.VMEM((4, wide), F32),
            pltpu.VMEM((heads, P_SIZE), F32),
            pltpu.VMEM((2 * chunks, 3 * Q // 2, RIM + Q // 2), BF16),
            pltpu.VMEM((Q, Q), F32),
            pltpu.VMEM((chunks, Q, Q), F32),
            pltpu.VMEM((chunks, Q // 128, 128), F32),
            pltpu.VMEM((2, RIM, wide), BF16),
            pltpu.VMEM((2, RIM, wide), BF16),
            pltpu.VMEM((2, RIM, wide), BF16),
            pltpu.VMEM((heads, 2, MESSAGE, P_SIZE), BF16),
            pltpu.VMEM((n_seq, 2, MESSAGE, P_SIZE), BF16),
            pltpu.VMEM((n_seq, 2, N, P_SIZE), BF16),
            (pltpu.VMEM((heads // SETS, 2, N, P_SIZE), BF16),) * SETS,
            pltpu.VMEM((n_head, chunks, Q // 128, 128), F32),
            dma(chunks), dma(chunks), dma(chunks), dma(2), dma(2), dma(2),
            dma(heads), dma(n_seq), dma(n_seq), dma(heads), dma(n_head), dma(n_head),
        ],
        compiler_params=pltpu.CompilerParams(
            vmem_limit_bytes=VMEM_MAIN * MIB,
            **(dict(collective_id=0, has_side_effects=True) if comm else {}),
        ),
        name="main",
    )(inputs, gates, *small, positions)


def norm_kernel(gated_hbm, scale_ref, gain_ref, out_hbm, rows, in_sem, out_sem):
    chunks = scale_ref.shape[0]

    def part(c):
        return pl.ds(c * Q, Q)

    def in_copy(c):
        return pltpu.make_async_copy(gated_hbm.at[part(c)], rows.at[part(c)], in_sem.at[c])

    def out_copy(c):
        return pltpu.make_async_copy(rows.at[part(c)], out_hbm.at[part(c)], out_sem.at[c])

    for c in range(chunks):
        in_copy(c).start()
    for c in range(chunks):
        scale = scale_ref[c]
        line = jnp.concatenate([scale[0:1], scale[1:2]], axis=1)
        col = jnp.transpose(jnp.broadcast_to(line, (128, Q)))
        in_copy(c).wait()
        for k in range(rows.shape[1] // 128):
            at = slice(k * 128, (k + 1) * 128)
            rows[part(c), at] = (rows[part(c), at].astype(F32) * col * gain_ref[:, at]).astype(BF16)
        out_copy(c).start()
    for c in range(chunks):
        out_copy(c).wait()


def norm_call(gated, scale, gain):
    tokens, width = gated.shape
    vmem = pl.BlockSpec(memory_space=pltpu.VMEM)
    hbm = pl.BlockSpec(memory_space=pl.ANY)
    return pl.pallas_call(
        norm_kernel,
        in_specs=[hbm, vmem, vmem],
        out_specs=hbm,
        out_shape=jax.ShapeDtypeStruct((tokens, width), BF16),
        scratch_shapes=[
            pltpu.VMEM((tokens, width), BF16),
            pltpu.SemaphoreType.DMA((tokens // Q,)), pltpu.SemaphoreType.DMA((tokens // Q,)),
        ],
        compiler_params=pltpu.CompilerParams(vmem_limit_bytes=60 * MIB),
        name="norm",
    )(gated, scale, gain)


def on_device(
    inputs, gates, writes, reads, step_raw, step_bias, decay_rate, skip_gain,
    conv_inputs, conv_writes, conv_reads, norm_gain, positions, segments,
    comm=True, phases=5,
):
    tokens, width = inputs.shape
    half_rows = tokens // 2
    n_seq = lax.axis_size("seq") if comm else 16
    n_head = lax.axis_size("head") if comm else 8
    small = (
        writes, reads, step_raw, step_bias[None], decay_rate[None], skip_gain[None],
        conv_inputs, conv_writes, conv_reads, segments.reshape(-1, half_rows // 128, 128),
    )
    gated, scale = main_call(n_seq, n_head, comm, phases, inputs, gates, small, positions)
    return norm_call(gated, scale, norm_gain[None])


def solution(mesh):
    return jax.shard_map(
        on_device,
        mesh=mesh,
        in_specs=(
            P("seq", "head"), P("seq", "head"), P("seq", "head"), P("seq", "head"), P("head", "seq"),
            P("head"), P("head"), P("head"), P(None, "head"), P(None, "head"), P(None, "head"),
            P("head"), P("seq"), P(),
        ),
        out_specs=P("seq", "head"),
        check_vma=False,
    )
```

```python
import functools

import jax
import jax.numpy as jnp
from jax import lax
from jax.experimental import pallas as pl
from jax.experimental.pallas import tpu as pltpu
from jax.sharding import PartitionSpec as P

H = 128
P_SIZE = 128
N = 128
G = 8
Q = 256
SETS = 4
VMEM_MAIN = 60
SCAN_AFTER_SENDING = ((), (), (0,), (1,))
SCAN_AFTER_INNER = {1: (2,), 4: (3,)}
EPSILON = 1e-05
LOG2E = 1.4426950408889634
MESH = pl.DeviceIdType.MESH
MIB = 2**20
F32 = jnp.float32
BF16 = jnp.bfloat16
RIM = 16


def silu_of_half(h):
    return h + h * jnp.tanh(h)


def spread_out(cols, lane, width=P_SIZE):
    return jnp.broadcast_to(cols[:, lane : lane + 1], (cols.shape[0], width))


def main_kernel(
    n_seq, n_head, comm, phases,
    x_hbm, gate_hbm, write_ref, read_ref, step_ref, bias_ref, rate_ref, skip_ref, ci_ref, cw_ref, cr_ref,
    seg_ref, pos_ref,
    out_hbm, scale_ref,
    raw, feats, gate, wct, wc, r_enter, r_half, cols, frow, trow, segs, decay, half_decay, loc_scale, half_scale,
    sloc, state, raw_group, taps, skips, shifts, upper, scores, sq, rim_own, rim_mine, rim_in,
    msg, recv, scanned, back, entering, whole, sums,
    x_sem, g_sem, o_sem, t_sem, h_send, h_recv, s1, r1, s2, r2, s3, r3,
):
    tokens, width = feats.shape
    heads = width // P_SIZE
    chunks = tokens // Q
    per_half = chunks // 2
    half_rows = tokens // 2
    per_set = heads // SETS
    set_width = per_set * P_SIZE
    side = Q // 2
    me = lax.axis_index("seq") if comm else 0
    my_head = lax.axis_index("head") if comm else 0
    slice_rows = N // n_seq
    block = 2 * slice_rows
    states_rows = per_set * block
    CUM, INFO = 0, heads
    first, second = pos_ref[0], pos_ref[half_rows]
    flip = jnp.where(first > second, 1, 0)

    def rows_of(c):
        return pl.ds(pl.multiple_of(c * Q, Q), Q)

    def lanes_of(start, count):
        return pl.ds(pl.multiple_of(start, P_SIZE), count)

    def window_of(c, rim):
        start = c * Q + (c // per_half) * RIM
        return pl.ds(pl.multiple_of(start if rim else start + RIM, RIM), Q + RIM if rim else Q)

    def x_copy(c):
        return pltpu.make_async_copy(x_hbm.at[rows_of(c)], raw.at[window_of(c, False)], x_sem.at[c])

    def gate_copy(c):
        return pltpu.make_async_copy(gate_hbm.at[rows_of(c)], gate.at[rows_of(c)], g_sem.at[c])

    def out_copy(c):
        return pltpu.make_async_copy(feats.at[rows_of(c)], out_hbm.at[rows_of(c)], o_sem.at[c])

    def tail_copy(k):
        end = half_rows * (k + 1)
        return pltpu.make_async_copy(
            x_hbm.at[pl.ds(end - RIM, RIM)], rim_own.at[k, :, pl.ds(0, width)], t_sem.at[k]
        )

    for k in (0, 1):
        tail_copy(k).start()
    for c in range(chunks):
        x_copy(c).start()
    for c in range(chunks):
        gate_copy(c).start()

    if comm:
        barrier = pltpu.get_barrier_semaphore()
        for k in range(1, n_seq):
            pl.semaphore_signal(barrier, inc=1, device_id={"seq": lax.rem(me + k, n_seq)}, device_id_type=MESH)
        for k in range(1, n_head):
            pl.semaphore_signal(barrier, inc=1, device_id={"head": lax.rem(my_head + k, n_head)}, device_id_type=MESH)

    for k in (0, 1):
        tail_copy(k).wait()
        end = half_rows * (k + 1)
        rim_own[k, :, width : width + N] = write_ref[end - RIM : end]
        rim_own[k, :, width + N :] = read_ref[end - RIM : end]
    rim_mine[0] = rim_own[flip]
    rim_mine[1] = rim_own[1 - flip]
    rim_copies = []
    if comm:
        pl.semaphore_wait(barrier, n_seq - 1 + n_head - 1)
        for k, to in ((0, lax.rem(me + 1, n_seq)), (1, lax.rem(me + n_seq - 1, n_seq))):
            rim_copies.append(
                pltpu.make_async_remote_copy(
                    src_ref=rim_mine.at[k], dst_ref=rim_in.at[k], send_sem=h_send.at[k],
                    recv_sem=h_recv.at[k], device_id={"seq": to}, device_id_type=MESH,
                )
            )
            rim_copies[-1].start()

    taps[:, :width] = ci_ref[...].astype(F32) * 0.5
    taps[:, width : width + N] = cw_ref[...].astype(F32) * 0.5
    taps[:, width + N :] = cr_ref[...].astype(F32) * 0.5
    state[...] = jnp.zeros_like(state)
    eye = lax.broadcasted_iota(jnp.int32, (heads, heads), 0) == lax.broadcasted_iota(jnp.int32, (heads, heads), 1)

    def column(ref):
        return jnp.sum(jnp.where(eye, jnp.broadcast_to(ref[...], (heads, heads)), 0.0), axis=1, keepdims=True)

    bias, rate = column(bias_ref), column(rate_ref) * -LOG2E
    skips[...] = jnp.broadcast_to(column(skip_ref), (heads, P_SIZE))
    lane = lax.broadcasted_iota(jnp.int32, (1, half_rows), 1)
    for k, start in ((0, first), (1, second)):
        at = start // half_rows

        def in_a_row(block):
            return jnp.concatenate([block[j : j + 1] for j in range(half_rows // 128)], axis=1).astype(F32)

        here = in_a_row(seg_ref[at])
        ahead = in_a_row(seg_ref[jnp.maximum(at - 1, 0)])
        ahead = jnp.where(jnp.full(ahead.shape, at, jnp.int32) > 0, ahead, -1.0)
        lines = [here]
        for ago in (1, 2, 3):
            lines.append(jnp.where(lane < ago, pltpu.roll(ahead, ago, 1), pltpu.roll(here, ago, 1)))
        for j, line in enumerate(lines):
            segs[j : j + 1, k * half_rows : (k + 1) * half_rows] = line

    row = lax.broadcasted_iota(jnp.int32, (Q, Q), 0)
    col = lax.broadcasted_iota(jnp.int32, (Q, Q), 1)
    upper[...] = jnp.where(row <= col, 1.0, 0.0).astype(F32)

    def by_chunk(one_of):
        return jnp.concatenate([one_of(c) for c in range(chunks)], axis=0)

    def chunk_lanes(c):
        return slice(c * Q, (c + 1) * Q)

    def prepare():
        raw_step = by_chunk(lambda c: step_ref[:, chunk_lanes(c)])
        step = jax.nn.softplus(raw_step + by_chunk(lambda c: bias))
        cum = jnp.dot(
            step * by_chunk(lambda c: rate), upper[...], precision=lax.Precision.HIGHEST, preferred_element_type=F32
        )
        cum_end = cum[:, Q - 1 : Q]
        middle = 0.5 * cum_end
        grown = jnp.exp2(cum - middle)
        factor = jnp.exp2(middle - cum) * step
        tail = jnp.exp2(cum_end - cum) * step
        wide = (heads, 128)
        for c in range(chunks):
            own = slice(c * heads, (c + 1) * heads)
            at = chunk_lanes(c)
            seg, one_ago = segs[0:1, at], segs[1:2, at]
            half_start = (c // per_half) * half_rows
            same = [jnp.where(seg == segs[k : k + 1, at], 1.0, 0.0) for k in (1, 2, 3)]
            enters = jnp.where(seg == one_ago[:, 0:1], 1.0, 0.0)
            enters_half = jnp.where(seg == segs[1:2, half_start : half_start + 1], 1.0, 0.0)
            leaves = jnp.where(seg == seg[:, Q - 1 : Q], 1.0, 0.0)
            base = jnp.zeros((heads, 1), F32) if c % per_half == 0 else base + end
            end, mid = cum_end[own], middle[own]
            frow[c] = factor[own]
            trow[c] = tail[own] * leaves
            decay[c] = jnp.broadcast_to(jnp.exp2(end) * enters[:, Q - 1 : Q], wide)
            half_decay[c] = jnp.broadcast_to(jnp.exp2(base + end) * enters_half[:, Q - 1 : Q], wide)
            loc_scale[c] = jnp.broadcast_to(jnp.exp2(mid), wide)
            half_scale[c] = jnp.broadcast_to(jnp.exp2(base + mid), wide)
            fill = jnp.zeros((128 - heads - 6, Q), F32)
            cols[c * Q : (c + 1) * Q] = jnp.transpose(
                jnp.concatenate([grown[own], seg, *same, enters, enters_half, fill], axis=0)
            )

    if phases >= 1:
        prepare()

    if comm:
        for copy in rim_copies:
            copy.wait()
        rim_in[1] = jnp.where(
            jnp.full(rim_in.shape[1:], me) == n_seq - 1, rim_mine[0].astype(F32), rim_in[1].astype(F32)
        ).astype(BF16)
    for k, rim in ((0, rim_in[flip]), (1, rim_in[1 - flip])):
        start = k * (half_rows + RIM)
        raw[start : start + RIM] = rim[:, :width]
        raw_group[start : start + RIM] = rim[:, width:]
        for j, ref in ((0, write_ref), (1, read_ref)):
            raw_group[start + RIM : start + RIM + half_rows, j * N : (j + 1) * N] = ref[
                k * half_rows : (k + 1) * half_rows
            ]

    to_row = lax.broadcasted_iota(jnp.int32, (side, RIM + side), 0)
    from_row = lax.broadcasted_iota(jnp.int32, (side, RIM + side), 1)

    def conv(source, c, lanes, tap_lanes):
        tap = [taps[k : k + 1, tap_lanes] for k in range(4)]
        x = source[window_of(c, True), lanes]
        out = []
        for b in (0, 1):
            moved = jnp.dot(shifts[2 * c + b], x[b * side : RIM + (b + 1) * side], preferred_element_type=F32)
            total = x[RIM + b * side : RIM + (b + 1) * side].astype(F32) * tap[3]
            for k in (1, 2, 3):
                total = total + moved[(k - 1) * side : k * side] * tap[3 - k]
            out.append(silu_of_half(total))
        return jnp.concatenate(out, axis=0)

    def write_part(c, _):
        info = cols[rows_of(c)]
        for b in (0, 1):
            for k in (1, 2, 3):
                same = spread_out(info[b * side : (b + 1) * side], INFO + k, RIM + side)
                hit = jnp.where(from_row == to_row + (RIM - k), same, 0.0)
                shifts[2 * c + b, (k - 1) * side : k * side] = hit.astype(BF16)
        w = conv(raw_group, c, slice(0, N), slice(width, width + N)).astype(BF16)
        wc[rows_of(c)] = w
        wct[c] = jnp.transpose(w.astype(F32))
        return 0

    if phases >= 2:
        lax.fori_loop(0, chunks, write_part, 0, unroll=2)

    def read_part(c, _):
        info = cols[rows_of(c)]
        r = conv(raw_group, c, slice(N, 2 * N), slice(width + N, width + 2 * N)).astype(BF16)
        wide = r.astype(F32)
        r_enter[rows_of(c)] = (wide * spread_out(info, INFO + 4)).astype(BF16)
        r_half[rows_of(c)] = (wide * spread_out(info, INFO + 5)).astype(BF16)
        full = lax.dot_general(r, wc[rows_of(c)], (((1,), (1,)), ((), ())), preferred_element_type=F32)
        seg_row = segs[0:1, lanes_of(c * Q, Q)]
        keep = (info[:, INFO : INFO + 1] == seg_row) & (col <= row)
        scores[c] = jnp.where(keep, full, 0.0)
        return 0

    def conv_part(g, c, _):
        if g == 0:
            x_copy(c).wait()
        for pair in range(per_set // 2):
            start = g * set_width + pair * 2 * P_SIZE
            at = slice(start, start + 2 * P_SIZE)
            feats[rows_of(c), at] = conv(raw, c, at, at).astype(BF16)
        return 0

    def state_part(g, c, _):
        half = c // per_half
        w = wct[c]
        for h in range(g * per_set, (g + 1) * per_set):
            one = slice(h, h + 1)
            scaled = (w * trow[c, one, :]).astype(BF16)
            add = jnp.dot(scaled, feats[rows_of(c), h * P_SIZE : (h + 1) * P_SIZE], preferred_element_type=F32)
            old = state[half, h]
            sloc[c, h] = (old * loc_scale[c, one, :]).astype(BF16)
            state[half, h] = old * decay[c, one, :] + add
        return 0

    def state_copy(g, k, src):
        to = lax.rem(me + k, n_seq)
        return pltpu.make_async_remote_copy(
            src_ref=msg.at[g, to], dst_ref=recv.at[g, src], send_sem=s1.at[g * n_seq + k],
            recv_sem=r1.at[g * n_seq + k], device_id={"seq": to}, device_id_type=MESH,
        )

    def enter_copy(g, k, src):
        to = lax.rem(me + k, n_seq)
        return pltpu.make_async_remote_copy(
            src_ref=back.at[g, to], dst_ref=entering.at[g, src], send_sem=s2.at[g * n_seq + k],
            recv_sem=r2.at[g * n_seq + k], device_id={"seq": to}, device_id_type=MESH,
        )

    def behind(k):
        return lax.rem(me + n_seq - k, n_seq)

    def send_states(g):
        decays = []
        for j in range(per_set):
            h = g * per_set + j
            both = []
            for half in (flip, 1 - flip):
                both.append(state[half, h].reshape(n_seq, slice_rows, P_SIZE))
                kept = half_decay[(half + 1) * per_half - 1, h : h + 1]
                high = kept.astype(BF16).astype(F32)
                decays += [high, kept - high]
            msg[g, :, j * block : (j + 1) * block] = jnp.concatenate(both, axis=1).astype(BF16)
        lines = jnp.concatenate(decays, axis=0)
        msg[g, :, states_rows:] = jnp.broadcast_to(lines[None], (n_seq, *lines.shape)).astype(BF16)
        if comm:
            for k in range(1, n_seq):
                state_copy(g, k, me).start()
            recv[g, me] = msg[g, me]

    def scan_states(g):
        if not comm:
            return
        for k in range(1, n_seq):
            state_copy(g, k, behind(k)).wait_recv()

        def advance(totals, src, half):
            got = recv[g, src].astype(F32)
            new = []
            for j, total in enumerate(totals):
                at = j * block + half * slice_rows
                scanned[src, at : at + slice_rows] = total
                line = states_rows + 4 * j + 2 * half
                keep = got[line : line + 1] + got[line + 1 : line + 2]
                new.append(total * keep + got[at : at + slice_rows])
            return tuple(new)

        totals = tuple(jnp.zeros((slice_rows, P_SIZE), F32) for _ in range(per_set))
        totals = lax.fori_loop(0, n_seq, lambda k, t: advance(t, k, 0), totals, unroll=4)
        lax.fori_loop(0, n_seq, lambda k, t: advance(t, n_seq - 1 - k, 1), totals, unroll=4)
        back[g] = scanned[...].astype(BF16)
        for k in range(1, n_seq):
            enter_copy(g, k, me).start()
        entering[g, me] = back[g, me]

    def assemble(g):
        for j in range(per_set):
            h = g * per_set + j
            both = entering[g, :, j * block : (j + 1) * block].astype(F32)
            low = both[:, :slice_rows].reshape(N, P_SIZE)
            high = both[:, slice_rows:].reshape(N, P_SIZE)
            swap = jnp.full(low.shape, flip) > 0
            whole[0, h] = jnp.where(swap, high, low).astype(BF16)
            whole[1, h] = jnp.where(swap, low, high).astype(BF16)

    if phases >= 3:
        for g in range(SETS):
            lax.fori_loop(0, chunks, functools.partial(conv_part, g), 0, unroll=2)
            lax.fori_loop(0, chunks, functools.partial(state_part, g), 0, unroll=4)
            send_states(g)
            for ready in SCAN_AFTER_SENDING[g]:
                scan_states(ready)

    def inner_part(c, _):
        info = cols[rows_of(c)]
        gate_copy(c).wait()

        masked = scores[c]
        r = r_enter[rows_of(c)]
        for h in range(heads):
            one = slice(h * P_SIZE, (h + 1) * P_SIZE)
            feat = feats[rows_of(c), one]
            fac = frow[c, h : h + 1, :]
            top = jnp.concatenate([r[:side], (masked[:side, :side] * fac[:, :side]).astype(BF16)], axis=1)
            low = jnp.concatenate([r[side:], (masked[side:] * fac).astype(BF16)], axis=1)
            entry = sloc[c, h]
            y = jnp.concatenate(
                [
                    jnp.dot(top, jnp.concatenate([entry, feat[:side]], axis=0), preferred_element_type=F32),
                    jnp.dot(low, jnp.concatenate([entry, feat], axis=0), preferred_element_type=F32),
                ],
                axis=0,
            )
            grown = spread_out(info, CUM + h)
            opened = silu_of_half(gate[rows_of(c), one].astype(F32) * 0.5)
            y = (y * grown + feat.astype(F32) * skips[h : h + 1, :]) * opened
            gate[rows_of(c), one] = (grown * opened).astype(BF16)
            raw[rows_of(c), one] = y.astype(BF16)
        return 0

    if phases >= 4:
        lax.fori_loop(0, chunks, read_part, 0, unroll=2)
        done = 0
        for until, ready in [*SCAN_AFTER_INNER.items(), (chunks, ())]:
            lax.fori_loop(done, until, inner_part, 0)
            done = until
            for g in ready:
                scan_states(g)

    def finish_part(c, _):
        r = r_half[rows_of(c)]
        half = c // per_half
        total = jnp.zeros((Q, P_SIZE), F32)
        for pair in range(heads // 2):
            states = []
            for h in (2 * pair, 2 * pair + 1):
                state_in = whole[half, h].astype(F32)
                states.append((state_in * half_scale[c, h : h + 1, :]).astype(BF16))
            inter = jnp.dot(r, jnp.concatenate(states, axis=1), preferred_element_type=F32)
            for j in (0, 1):
                start = (2 * pair + j) * P_SIZE
                one = slice(start, start + P_SIZE)
                gated = raw[rows_of(c), one].astype(F32)
                gated = gated + inter[:, j * P_SIZE : (j + 1) * P_SIZE] * gate[rows_of(c), one].astype(F32)
                total = total + gated * gated
                feats[rows_of(c), one] = gated.astype(BF16)
        out_copy(c).start()
        sums_here = jnp.sum(jnp.transpose(total), axis=0, keepdims=True)
        sq[c] = jnp.concatenate([sums_here[:, :128], sums_here[:, 128:]], axis=0)
        return 0

    for g in range(SETS):
        if comm:
            for k in range(1, n_seq):
                enter_copy(g, k, behind(k)).wait_recv()
        assemble(g)

    if phases >= 5:
        lax.fori_loop(0, chunks, finish_part, 0)

    total = sq[...]
    if comm:
        copies = []
        for k in range(1, n_head):
            copies.append(
                pltpu.make_async_remote_copy(
                    src_ref=sq, dst_ref=sums.at[k], send_sem=s3.at[k], recv_sem=r3.at[k],
                    device_id={"head": lax.rem(my_head + k, n_head)}, device_id_type=MESH,
                )
            )
            copies[-1].start()
        for g in range(SETS):
            for k in range(1, n_seq):
                state_copy(g, k, me).wait_send()
                enter_copy(g, k, me).wait_send()
        for k in range(1, n_head):
            copies[k - 1].wait()
            total = total + sums[k]
    scale_ref[...] = lax.rsqrt(total / (H * P_SIZE) + EPSILON)
    if phases >= 5:
        for c in range(chunks):
            out_copy(c).wait()
    if phases < 4:
        for c in range(chunks):
            gate_copy(c).wait()
    if phases < 3:
        for c in range(chunks):
            x_copy(c).wait()


def main_call(n_seq, n_head, comm, phases, inputs, gates, small, positions):
    tokens, width = inputs.shape
    heads = width // P_SIZE
    chunks = tokens // Q
    wide = width + 2 * N
    rows = heads // SETS * 2 * N // n_seq
    vmem = pl.BlockSpec(memory_space=pltpu.VMEM)
    hbm = pl.BlockSpec(memory_space=pl.ANY)
    dma = lambda n: pltpu.SemaphoreType.DMA((n,))
    return pl.pallas_call(
        functools.partial(main_kernel, n_seq, n_head, comm, phases),
        in_specs=[hbm, hbm] + [vmem] * len(small) + [pl.BlockSpec(memory_space=pltpu.SMEM)],
        out_specs=[hbm, vmem],
        out_shape=[
            jax.ShapeDtypeStruct((tokens, width), BF16),
            jax.ShapeDtypeStruct((chunks, Q // 128, 128), F32),
        ],
        scratch_shapes=[
            pltpu.VMEM((tokens + 2 * RIM, width), BF16),
            pltpu.VMEM((tokens, width), BF16),
            pltpu.VMEM((tokens, width), BF16),
            pltpu.VMEM((chunks, N, Q), F32),
            pltpu.VMEM((tokens, N), BF16),
            pltpu.VMEM((tokens, N), BF16),
            pltpu.VMEM((tokens, N), BF16),
            pltpu.VMEM((tokens, 128), F32),
            pltpu.VMEM((chunks, heads, Q), F32),
            pltpu.VMEM((chunks, heads, Q), F32),
            pltpu.VMEM((8, tokens), F32),
            pltpu.VMEM((chunks, heads, 128), F32),
            pltpu.VMEM((chunks, heads, 128), F32),
            pltpu.VMEM((chunks, heads, 128), F32),
            pltpu.VMEM((chunks, heads, 128), F32),
            pltpu.VMEM((chunks, heads, N, P_SIZE), BF16),
            pltpu.VMEM((2, heads, N, P_SIZE), F32),
            pltpu.VMEM((tokens + 2 * RIM, 2 * N), BF16),
            pltpu.VMEM((4, wide), F32),
            pltpu.VMEM((heads, P_SIZE), F32),
            pltpu.VMEM((2 * chunks, 3 * Q // 2, RIM + Q // 2), BF16),
            pltpu.VMEM((Q, Q), F32),
            pltpu.VMEM((chunks, Q, Q), F32),
            pltpu.VMEM((chunks, Q // 128, 128), F32),
            pltpu.VMEM((2, RIM, wide), BF16),
            pltpu.VMEM((2, RIM, wide), BF16),
            pltpu.VMEM((2, RIM, wide), BF16),
            pltpu.VMEM((SETS, n_seq, rows + 16, P_SIZE), BF16),
            pltpu.VMEM((SETS, n_seq, rows + 16, P_SIZE), BF16),
            pltpu.VMEM((n_seq, rows, P_SIZE), F32),
            pltpu.VMEM((SETS, n_seq, rows, P_SIZE), BF16),
            pltpu.VMEM((SETS, n_seq, rows, P_SIZE), BF16),
            pltpu.VMEM((2, heads, N, P_SIZE), BF16),
            pltpu.VMEM((n_head, chunks, Q // 128, 128), F32),
            dma(chunks), dma(chunks), dma(chunks), dma(2), dma(2), dma(2),
            *[dma(SETS * n_seq)] * 4, dma(n_head), dma(n_head),
        ],
        compiler_params=pltpu.CompilerParams(
            vmem_limit_bytes=VMEM_MAIN * MIB,
            **(dict(collective_id=0, has_side_effects=True) if comm else {}),
        ),
        name="main",
    )(inputs, gates, *small, positions)


def norm_kernel(gated_hbm, scale_ref, gain_ref, out_hbm, rows, in_sem, out_sem):
    chunks = scale_ref.shape[0]

    def part(c):
        return pl.ds(c * Q, Q)

    def in_copy(c):
        return pltpu.make_async_copy(gated_hbm.at[part(c)], rows.at[part(c)], in_sem.at[c])

    def out_copy(c):
        return pltpu.make_async_copy(rows.at[part(c)], out_hbm.at[part(c)], out_sem.at[c])

    for c in range(chunks):
        in_copy(c).start()
    for c in range(chunks):
        scale = scale_ref[c]
        line = jnp.concatenate([scale[0:1], scale[1:2]], axis=1)
        col = jnp.transpose(jnp.broadcast_to(line, (128, Q)))
        in_copy(c).wait()
        for k in range(rows.shape[1] // 128):
            at = slice(k * 128, (k + 1) * 128)
            rows[part(c), at] = (rows[part(c), at].astype(F32) * col * gain_ref[:, at]).astype(BF16)
        out_copy(c).start()
    for c in range(chunks):
        out_copy(c).wait()


def norm_call(gated, scale, gain):
    tokens, width = gated.shape
    vmem = pl.BlockSpec(memory_space=pltpu.VMEM)
    hbm = pl.BlockSpec(memory_space=pl.ANY)
    return pl.pallas_call(
        norm_kernel,
        in_specs=[hbm, vmem, vmem],
        out_specs=hbm,
        out_shape=jax.ShapeDtypeStruct((tokens, width), BF16),
        scratch_shapes=[
            pltpu.VMEM((tokens, width), BF16),
            pltpu.SemaphoreType.DMA((tokens // Q,)), pltpu.SemaphoreType.DMA((tokens // Q,)),
        ],
        compiler_params=pltpu.CompilerParams(vmem_limit_bytes=60 * MIB),
        name="norm",
    )(gated, scale, gain)


def on_device(
    inputs, gates, writes, reads, step_raw, step_bias, decay_rate, skip_gain,
    conv_inputs, conv_writes, conv_reads, norm_gain, positions, segments,
    comm=True, phases=5,
):
    tokens, width = inputs.shape
    half_rows = tokens // 2
    n_seq = lax.axis_size("seq") if comm else 16
    n_head = lax.axis_size("head") if comm else 8
    small = (
        writes, reads, step_raw, step_bias[None], decay_rate[None], skip_gain[None],
        conv_inputs, conv_writes, conv_reads, segments.reshape(-1, half_rows // 128, 128),
    )
    gated, scale = main_call(n_seq, n_head, comm, phases, inputs, gates, small, positions)
    return norm_call(gated, scale, norm_gain[None])


def solution(mesh):
    return jax.shard_map(
        on_device,
        mesh=mesh,
        in_specs=(
            P("seq", "head"), P("seq", "head"), P("seq", "head"), P("seq", "head"), P("head", "seq"),
            P("head"), P("head"), P("head"), P(None, "head"), P(None, "head"), P(None, "head"),
            P("head"), P("seq"), P(),
        ),
        out_specs=P("seq", "head"),
        check_vma=False,
    )
```

```python
import functools

import jax
import jax.numpy as jnp
from jax import lax
from jax.experimental import pallas as pl
from jax.experimental.pallas import tpu as pltpu
from jax.sharding import PartitionSpec as P

H = 128
P_SIZE = 128
N = 128
G = 8
Q = 256
SETS = 4
VMEM_MAIN = 60
SCAN_AFTER_SENDING = ((), (), (0,), (1,))
SCAN_AFTER_INNER = {1: (2,), 4: (3,)}
EPSILON = 1e-05
LOG2E = 1.4426950408889634
MESH = pl.DeviceIdType.MESH
MIB = 2**20
F32 = jnp.float32
BF16 = jnp.bfloat16
RIM = 16


def silu_of_half(h):
    return h + h * jnp.tanh(h)


def spread_out(cols, lane, width=P_SIZE):
    return jnp.broadcast_to(cols[:, lane : lane + 1], (cols.shape[0], width))


def main_kernel(
    n_seq, n_head, comm, phases,
    x_hbm, gate_hbm, write_ref, read_ref, step_ref, bias_ref, rate_ref, skip_ref, ci_ref, cw_ref, cr_ref,
    seg_ref, pos_ref,
    out_hbm, scale_ref,
    raw, feats, gate, wct, wc, r_enter, r_half, cols, frow, trow, segs, decay, half_decay, loc_scale, half_scale,
    sloc, state, raw_group, taps, skips, shifts, upper, scores, sq, rim_own, rim_mine, rim_in,
    msg, recv, scanned, back, entering, whole, sums,
    x_sem, g_sem, o_sem, t_sem, h_send, h_recv, s1, r1, s2, r2, s3, r3,
):
    tokens, width = feats.shape
    heads = width // P_SIZE
    chunks = tokens // Q
    per_half = chunks // 2
    half_rows = tokens // 2
    per_set = heads // SETS
    set_width = per_set * P_SIZE
    side = Q // 2
    me = lax.axis_index("seq") if comm else 0
    my_head = lax.axis_index("head") if comm else 0
    slice_rows = N // n_seq
    block = 2 * slice_rows
    states_rows = per_set * block
    CUM, INFO = 0, heads
    first, second = pos_ref[0], pos_ref[half_rows]
    flip = jnp.where(first > second, 1, 0)

    def rows_of(c):
        return pl.ds(pl.multiple_of(c * Q, Q), Q)

    def lanes_of(start, count):
        return pl.ds(pl.multiple_of(start, P_SIZE), count)

    def window_of(c, rim):
        start = c * Q + (c // per_half) * RIM
        return pl.ds(pl.multiple_of(start if rim else start + RIM, RIM), Q + RIM if rim else Q)

    def x_copy(c):
        return pltpu.make_async_copy(x_hbm.at[rows_of(c)], raw.at[window_of(c, False)], x_sem.at[c])

    def gate_copy(c):
        return pltpu.make_async_copy(gate_hbm.at[rows_of(c)], gate.at[rows_of(c)], g_sem.at[c])

    def out_copy(c):
        return pltpu.make_async_copy(feats.at[rows_of(c)], out_hbm.at[rows_of(c)], o_sem.at[c])

    def tail_copy(k):
        end = half_rows * (k + 1)
        return pltpu.make_async_copy(
            x_hbm.at[pl.ds(end - RIM, RIM)], rim_own.at[k, :, pl.ds(0, width)], t_sem.at[k]
        )

    for k in (0, 1):
        tail_copy(k).start()
    for c in range(chunks):
        x_copy(c).start()
    for c in range(chunks):
        gate_copy(c).start()

    if comm:
        barrier = pltpu.get_barrier_semaphore()
        for k in range(1, n_seq):
            pl.semaphore_signal(barrier, inc=1, device_id={"seq": lax.rem(me + k, n_seq)}, device_id_type=MESH)
        for k in range(1, n_head):
            pl.semaphore_signal(barrier, inc=1, device_id={"head": lax.rem(my_head + k, n_head)}, device_id_type=MESH)

    for k in (0, 1):
        tail_copy(k).wait()
        end = half_rows * (k + 1)
        rim_own[k, :, width : width + N] = write_ref[end - RIM : end]
        rim_own[k, :, width + N :] = read_ref[end - RIM : end]
    rim_mine[0] = rim_own[flip]
    rim_mine[1] = rim_own[1 - flip]
    rim_copies = []
    if comm:
        pl.semaphore_wait(barrier, n_seq - 1 + n_head - 1)
        for k, to in ((0, lax.rem(me + 1, n_seq)), (1, lax.rem(me + n_seq - 1, n_seq))):
            rim_copies.append(
                pltpu.make_async_remote_copy(
                    src_ref=rim_mine.at[k], dst_ref=rim_in.at[k], send_sem=h_send.at[k],
                    recv_sem=h_recv.at[k], device_id={"seq": to}, device_id_type=MESH,
                )
            )
            rim_copies[-1].start()

    taps[:, :width] = ci_ref[...].astype(F32) * 0.5
    taps[:, width : width + N] = cw_ref[...].astype(F32) * 0.5
    taps[:, width + N :] = cr_ref[...].astype(F32) * 0.5
    state[...] = jnp.zeros_like(state)
    eye = lax.broadcasted_iota(jnp.int32, (heads, heads), 0) == lax.broadcasted_iota(jnp.int32, (heads, heads), 1)

    def column(ref):
        return jnp.sum(jnp.where(eye, jnp.broadcast_to(ref[...], (heads, heads)), 0.0), axis=1, keepdims=True)

    bias, rate = column(bias_ref), column(rate_ref) * -LOG2E
    skips[...] = jnp.broadcast_to(column(skip_ref), (heads, P_SIZE))
    lane = lax.broadcasted_iota(jnp.int32, (1, half_rows), 1)
    for k, start in ((0, first), (1, second)):
        at = start // half_rows

        def in_a_row(block):
            return jnp.concatenate([block[j : j + 1] for j in range(half_rows // 128)], axis=1).astype(F32)

        here = in_a_row(seg_ref[at])
        ahead = in_a_row(seg_ref[jnp.maximum(at - 1, 0)])
        ahead = jnp.where(jnp.full(ahead.shape, at, jnp.int32) > 0, ahead, -1.0)
        lines = [here]
        for ago in (1, 2, 3):
            lines.append(jnp.where(lane < ago, pltpu.roll(ahead, ago, 1), pltpu.roll(here, ago, 1)))
        for j, line in enumerate(lines):
            segs[j : j + 1, k * half_rows : (k + 1) * half_rows] = line

    row = lax.broadcasted_iota(jnp.int32, (Q, Q), 0)
    col = lax.broadcasted_iota(jnp.int32, (Q, Q), 1)
    upper[...] = jnp.where(row <= col, 1.0, 0.0).astype(F32)

    def by_chunk(one_of):
        return jnp.concatenate([one_of(c) for c in range(chunks)], axis=0)

    def chunk_lanes(c):
        return slice(c * Q, (c + 1) * Q)

    def prepare():
        raw_step = by_chunk(lambda c: step_ref[:, chunk_lanes(c)])
        step = jax.nn.softplus(raw_step + by_chunk(lambda c: bias))
        cum = jnp.dot(
            step * by_chunk(lambda c: rate), upper[...], precision=lax.Precision.HIGHEST, preferred_element_type=F32
        )
        cum_end = cum[:, Q - 1 : Q]
        middle = 0.5 * cum_end
        grown = jnp.exp2(cum - middle)
        factor = jnp.exp2(middle - cum) * step
        tail = jnp.exp2(cum_end - cum) * step
        wide = (heads, 128)
        for c in range(chunks):
            own = slice(c * heads, (c + 1) * heads)
            at = chunk_lanes(c)
            seg, one_ago = segs[0:1, at], segs[1:2, at]
            half_start = (c // per_half) * half_rows
            same = [jnp.where(seg == segs[k : k + 1, at], 1.0, 0.0) for k in (1, 2, 3)]
            enters = jnp.where(seg == one_ago[:, 0:1], 1.0, 0.0)
            enters_half = jnp.where(seg == segs[1:2, half_start : half_start + 1], 1.0, 0.0)
            leaves = jnp.where(seg == seg[:, Q - 1 : Q], 1.0, 0.0)
            base = jnp.zeros((heads, 1), F32) if c % per_half == 0 else base + end
            end, mid = cum_end[own], middle[own]
            frow[c] = factor[own]
            trow[c] = tail[own] * leaves
            decay[c] = jnp.broadcast_to(jnp.exp2(end) * enters[:, Q - 1 : Q], wide)
            half_decay[c] = jnp.broadcast_to(jnp.exp2(base + end) * enters_half[:, Q - 1 : Q], wide)
            loc_scale[c] = jnp.broadcast_to(jnp.exp2(mid), wide)
            half_scale[c] = jnp.broadcast_to(jnp.exp2(base + mid), wide)
            fill = jnp.zeros((128 - heads - 6, Q), F32)
            cols[c * Q : (c + 1) * Q] = jnp.transpose(
                jnp.concatenate([grown[own], seg, *same, enters, enters_half, fill], axis=0)
            )

    if phases >= 1:
        prepare()

    if comm:
        for copy in rim_copies:
            copy.wait()
        rim_in[1] = jnp.where(
            jnp.full(rim_in.shape[1:], me) == n_seq - 1, rim_mine[0].astype(F32), rim_in[1].astype(F32)
        ).astype(BF16)
    for k, rim in ((0, rim_in[flip]), (1, rim_in[1 - flip])):
        start = k * (half_rows + RIM)
        raw[start : start + RIM] = rim[:, :width]
        raw_group[start : start + RIM] = rim[:, width:]
        for j, ref in ((0, write_ref), (1, read_ref)):
            raw_group[start + RIM : start + RIM + half_rows, j * N : (j + 1) * N] = ref[
                k * half_rows : (k + 1) * half_rows
            ]

    to_row = lax.broadcasted_iota(jnp.int32, (side, RIM + side), 0)
    from_row = lax.broadcasted_iota(jnp.int32, (side, RIM + side), 1)

    def conv(source, c, lanes, tap_lanes):
        tap = [taps[k : k + 1, tap_lanes] for k in range(4)]
        x = source[window_of(c, True), lanes]
        out = []
        for b in (0, 1):
            moved = jnp.dot(shifts[2 * c + b], x[b * side : RIM + (b + 1) * side], preferred_element_type=F32)
            total = x[RIM + b * side : RIM + (b + 1) * side].astype(F32) * tap[3]
            for k in (1, 2, 3):
                total = total + moved[(k - 1) * side : k * side] * tap[3 - k]
            out.append(silu_of_half(total))
        return jnp.concatenate(out, axis=0)

    def write_part(c, _):
        info = cols[rows_of(c)]
        for b in (0, 1):
            for k in (1, 2, 3):
                same = spread_out(info[b * side : (b + 1) * side], INFO + k, RIM + side)
                hit = jnp.where(from_row == to_row + (RIM - k), same, 0.0)
                shifts[2 * c + b, (k - 1) * side : k * side] = hit.astype(BF16)
        w = conv(raw_group, c, slice(0, N), slice(width, width + N)).astype(BF16)
        wc[rows_of(c)] = w
        wct[c] = jnp.transpose(w.astype(F32))
        return 0

    if phases >= 2:
        lax.fori_loop(0, chunks, write_part, 0, unroll=2)

    def read_part(c, _):
        info = cols[rows_of(c)]
        r = conv(raw_group, c, slice(N, 2 * N), slice(width + N, width + 2 * N)).astype(BF16)
        wide = r.astype(F32)
        r_enter[rows_of(c)] = (wide * spread_out(info, INFO + 4)).astype(BF16)
        r_half[rows_of(c)] = (wide * spread_out(info, INFO + 5)).astype(BF16)
        full = lax.dot_general(r, wc[rows_of(c)], (((1,), (1,)), ((), ())), preferred_element_type=F32)
        seg_row = segs[0:1, lanes_of(c * Q, Q)]
        keep = (info[:, INFO : INFO + 1] == seg_row) & (col <= row)
        scores[c] = jnp.where(keep, full, 0.0)
        return 0

    def conv_part(g, c, _):
        if g == 0:
            x_copy(c).wait()
        for pair in range(per_set // 2):
            start = g * set_width + pair * 2 * P_SIZE
            at = slice(start, start + 2 * P_SIZE)
            feats[rows_of(c), at] = conv(raw, c, at, at).astype(BF16)
        return 0

    def state_part(g, c, _):
        half = c // per_half
        w = wct[c]
        for h in range(g * per_set, (g + 1) * per_set):
            one = slice(h, h + 1)
            scaled = (w * trow[c, one, :]).astype(BF16)
            add = jnp.dot(scaled, feats[rows_of(c), h * P_SIZE : (h + 1) * P_SIZE], preferred_element_type=F32)
            old = state[half, h]
            sloc[c, h] = (old * loc_scale[c, one, :]).astype(BF16)
            state[half, h] = old * decay[c, one, :] + add
        return 0

    def state_copy(g, k):
        to = lax.rem(me + k, n_seq)
        return pltpu.make_async_remote_copy(
            src_ref=msg.at[g, to], dst_ref=recv.at[g, me], send_sem=s1.at[g], recv_sem=r1.at[g],
            device_id={"seq": to}, device_id_type=MESH,
        )

    def all_states(g):
        others = pl.ds(0, n_seq - 1)
        return pltpu.make_async_remote_copy(
            src_ref=msg.at[g, others], dst_ref=recv.at[g, others], send_sem=s1.at[g],
            recv_sem=r1.at[g], device_id={"seq": lax.rem(me + 1, n_seq)}, device_id_type=MESH,
        )

    def all_entering(g):
        others = pl.ds(0, n_seq - 1)
        return pltpu.make_async_remote_copy(
            src_ref=back.at[g, others], dst_ref=entering.at[g, others], send_sem=s2.at[g],
            recv_sem=r2.at[g], device_id={"seq": lax.rem(me + 1, n_seq)}, device_id_type=MESH,
        )

    def enter_copy(g, k):
        to = lax.rem(me + k, n_seq)
        return pltpu.make_async_remote_copy(
            src_ref=back.at[g, to], dst_ref=entering.at[g, me], send_sem=s2.at[g], recv_sem=r2.at[g],
            device_id={"seq": to}, device_id_type=MESH,
        )

    def send_states(g):
        decays = []
        for j in range(per_set):
            h = g * per_set + j
            both = []
            for half in (flip, 1 - flip):
                both.append(state[half, h].reshape(n_seq, slice_rows, P_SIZE))
                kept = half_decay[(half + 1) * per_half - 1, h : h + 1]
                high = kept.astype(BF16).astype(F32)
                decays += [high, kept - high]
            msg[g, :, j * block : (j + 1) * block] = jnp.concatenate(both, axis=1).astype(BF16)
        lines = jnp.concatenate(decays, axis=0)
        msg[g, :, states_rows:] = jnp.broadcast_to(lines[None], (n_seq, *lines.shape)).astype(BF16)
        if comm:
            for k in range(1, n_seq):
                state_copy(g, k).start()
            recv[g, me] = msg[g, me]

    def scan_states(g):
        if not comm:
            return
        all_states(g).wait_recv()

        def advance(totals, src, half):
            got = recv[g, src].astype(F32)
            new = []
            for j, total in enumerate(totals):
                at = j * block + half * slice_rows
                scanned[src, at : at + slice_rows] = total
                line = states_rows + 4 * j + 2 * half
                keep = got[line : line + 1] + got[line + 1 : line + 2]
                new.append(total * keep + got[at : at + slice_rows])
            return tuple(new)

        totals = tuple(jnp.zeros((slice_rows, P_SIZE), F32) for _ in range(per_set))
        totals = lax.fori_loop(0, n_seq, lambda k, t: advance(t, k, 0), totals, unroll=4)
        lax.fori_loop(0, n_seq, lambda k, t: advance(t, n_seq - 1 - k, 1), totals, unroll=4)
        back[g] = scanned[...].astype(BF16)
        for k in range(1, n_seq):
            enter_copy(g, k).start()
        entering[g, me] = back[g, me]

    def assemble(g):
        for j in range(per_set):
            h = g * per_set + j
            both = entering[g, :, j * block : (j + 1) * block].astype(F32)
            low = both[:, :slice_rows].reshape(N, P_SIZE)
            high = both[:, slice_rows:].reshape(N, P_SIZE)
            swap = jnp.full(low.shape, flip) > 0
            whole[0, h] = jnp.where(swap, high, low).astype(BF16)
            whole[1, h] = jnp.where(swap, low, high).astype(BF16)

    if phases >= 3:
        for g in range(SETS):
            lax.fori_loop(0, chunks, functools.partial(conv_part, g), 0, unroll=2)
            lax.fori_loop(0, chunks, functools.partial(state_part, g), 0, unroll=4)
            send_states(g)
            for ready in SCAN_AFTER_SENDING[g]:
                scan_states(ready)

    def inner_part(c, _):
        info = cols[rows_of(c)]
        gate_copy(c).wait()

        masked = scores[c]
        r = r_enter[rows_of(c)]
        for h in range(heads):
            one = slice(h * P_SIZE, (h + 1) * P_SIZE)
            feat = feats[rows_of(c), one]
            fac = frow[c, h : h + 1, :]
            top = jnp.concatenate([r[:side], (masked[:side, :side] * fac[:, :side]).astype(BF16)], axis=1)
            low = jnp.concatenate([r[side:], (masked[side:] * fac).astype(BF16)], axis=1)
            entry = sloc[c, h]
            y = jnp.concatenate(
                [
                    jnp.dot(top, jnp.concatenate([entry, feat[:side]], axis=0), preferred_element_type=F32),
                    jnp.dot(low, jnp.concatenate([entry, feat], axis=0), preferred_element_type=F32),
                ],
                axis=0,
            )
            grown = spread_out(info, CUM + h)
            opened = silu_of_half(gate[rows_of(c), one].astype(F32) * 0.5)
            y = (y * grown + feat.astype(F32) * skips[h : h + 1, :]) * opened
            gate[rows_of(c), one] = (grown * opened).astype(BF16)
            raw[rows_of(c), one] = y.astype(BF16)
        return 0

    if phases >= 4:
        lax.fori_loop(0, chunks, read_part, 0, unroll=2)
        done = 0
        for until, ready in [*SCAN_AFTER_INNER.items(), (chunks, ())]:
            lax.fori_loop(done, until, inner_part, 0)
            done = until
            for g in ready:
                scan_states(g)

    def finish_part(c, _):
        r = r_half[rows_of(c)]
        half = c // per_half
        total = jnp.zeros((Q, P_SIZE), F32)
        for pair in range(heads // 2):
            states = []
            for h in (2 * pair, 2 * pair + 1):
                state_in = whole[half, h].astype(F32)
                states.append((state_in * half_scale[c, h : h + 1, :]).astype(BF16))
            inter = jnp.dot(r, jnp.concatenate(states, axis=1), preferred_element_type=F32)
            for j in (0, 1):
                start = (2 * pair + j) * P_SIZE
                one = slice(start, start + P_SIZE)
                gated = raw[rows_of(c), one].astype(F32)
                gated = gated + inter[:, j * P_SIZE : (j + 1) * P_SIZE] * gate[rows_of(c), one].astype(F32)
                total = total + gated * gated
                feats[rows_of(c), one] = gated.astype(BF16)
        out_copy(c).start()
        sums_here = jnp.sum(jnp.transpose(total), axis=0, keepdims=True)
        sq[c] = jnp.concatenate([sums_here[:, :128], sums_here[:, 128:]], axis=0)
        return 0

    for g in range(SETS):
        if comm:
            all_entering(g).wait_recv()
        assemble(g)

    if phases >= 5:
        lax.fori_loop(0, chunks, finish_part, 0)

    total = sq[...]
    if comm:
        copies = []
        for k in range(1, n_head):
            copies.append(
                pltpu.make_async_remote_copy(
                    src_ref=sq, dst_ref=sums.at[k], send_sem=s3.at[k], recv_sem=r3.at[k],
                    device_id={"head": lax.rem(my_head + k, n_head)}, device_id_type=MESH,
                )
            )
            copies[-1].start()
        for g in range(SETS):
            all_states(g).wait_send()
            all_entering(g).wait_send()
        for k in range(1, n_head):
            copies[k - 1].wait()
            total = total + sums[k]
    scale_ref[...] = lax.rsqrt(total / (H * P_SIZE) + EPSILON)
    if phases >= 5:
        for c in range(chunks):
            out_copy(c).wait()
    if phases < 4:
        for c in range(chunks):
            gate_copy(c).wait()
    if phases < 3:
        for c in range(chunks):
            x_copy(c).wait()


def main_call(n_seq, n_head, comm, phases, inputs, gates, small, positions):
    tokens, width = inputs.shape
    heads = width // P_SIZE
    chunks = tokens // Q
    wide = width + 2 * N
    rows = heads // SETS * 2 * N // n_seq
    vmem = pl.BlockSpec(memory_space=pltpu.VMEM)
    hbm = pl.BlockSpec(memory_space=pl.ANY)
    dma = lambda n: pltpu.SemaphoreType.DMA((n,))
    return pl.pallas_call(
        functools.partial(main_kernel, n_seq, n_head, comm, phases),
        in_specs=[hbm, hbm] + [vmem] * len(small) + [pl.BlockSpec(memory_space=pltpu.SMEM)],
        out_specs=[hbm, vmem],
        out_shape=[
            jax.ShapeDtypeStruct((tokens, width), BF16),
            jax.ShapeDtypeStruct((chunks, Q // 128, 128), F32),
        ],
        scratch_shapes=[
            pltpu.VMEM((tokens + 2 * RIM, width), BF16),
            pltpu.VMEM((tokens, width), BF16),
            pltpu.VMEM((tokens, width), BF16),
            pltpu.VMEM((chunks, N, Q), F32),
            pltpu.VMEM((tokens, N), BF16),
            pltpu.VMEM((tokens, N), BF16),
            pltpu.VMEM((tokens, N), BF16),
            pltpu.VMEM((tokens, 128), F32),
            pltpu.VMEM((chunks, heads, Q), F32),
            pltpu.VMEM((chunks, heads, Q), F32),
            pltpu.VMEM((8, tokens), F32),
            pltpu.VMEM((chunks, heads, 128), F32),
            pltpu.VMEM((chunks, heads, 128), F32),
            pltpu.VMEM((chunks, heads, 128), F32),
            pltpu.VMEM((chunks, heads, 128), F32),
            pltpu.VMEM((chunks, heads, N, P_SIZE), BF16),
            pltpu.VMEM((2, heads, N, P_SIZE), F32),
            pltpu.VMEM((tokens + 2 * RIM, 2 * N), BF16),
            pltpu.VMEM((4, wide), F32),
            pltpu.VMEM((heads, P_SIZE), F32),
            pltpu.VMEM((2 * chunks, 3 * Q // 2, RIM + Q // 2), BF16),
            pltpu.VMEM((Q, Q), F32),
            pltpu.VMEM((chunks, Q, Q), F32),
            pltpu.VMEM((chunks, Q // 128, 128), F32),
            pltpu.VMEM((2, RIM, wide), BF16),
            pltpu.VMEM((2, RIM, wide), BF16),
            pltpu.VMEM((2, RIM, wide), BF16),
            pltpu.VMEM((SETS, n_seq, rows + 4 * heads // SETS, P_SIZE), BF16),
            pltpu.VMEM((SETS, n_seq, rows + 4 * heads // SETS, P_SIZE), BF16),
            pltpu.VMEM((n_seq, rows, P_SIZE), F32),
            pltpu.VMEM((SETS, n_seq, rows, P_SIZE), BF16),
            pltpu.VMEM((SETS, n_seq, rows, P_SIZE), BF16),
            pltpu.VMEM((2, heads, N, P_SIZE), BF16),
            pltpu.VMEM((n_head, chunks, Q // 128, 128), F32),
            dma(chunks), dma(chunks), dma(chunks), dma(2), dma(2), dma(2),
            *[dma(SETS)] * 4, dma(n_head), dma(n_head),
        ],
        compiler_params=pltpu.CompilerParams(
            vmem_limit_bytes=VMEM_MAIN * MIB,
            **(dict(collective_id=0, has_side_effects=True) if comm else {}),
        ),
        name="main",
    )(inputs, gates, *small, positions)


def norm_kernel(gated_hbm, scale_ref, gain_ref, out_hbm, rows, in_sem, out_sem):
    chunks = scale_ref.shape[0]

    def part(c):
        return pl.ds(c * Q, Q)

    def in_copy(c):
        return pltpu.make_async_copy(gated_hbm.at[part(c)], rows.at[part(c)], in_sem.at[c])

    def out_copy(c):
        return pltpu.make_async_copy(rows.at[part(c)], out_hbm.at[part(c)], out_sem.at[c])

    for c in range(chunks):
        in_copy(c).start()
    for c in range(chunks):
        scale = scale_ref[c]
        line = jnp.concatenate([scale[0:1], scale[1:2]], axis=1)
        col = jnp.transpose(jnp.broadcast_to(line, (128, Q)))
        in_copy(c).wait()
        for k in range(rows.shape[1] // 128):
            at = slice(k * 128, (k + 1) * 128)
            rows[part(c), at] = (rows[part(c), at].astype(F32) * col * gain_ref[:, at]).astype(BF16)
        out_copy(c).start()
    for c in range(chunks):
        out_copy(c).wait()


def norm_call(gated, scale, gain):
    tokens, width = gated.shape
    vmem = pl.BlockSpec(memory_space=pltpu.VMEM)
    hbm = pl.BlockSpec(memory_space=pl.ANY)
    return pl.pallas_call(
        norm_kernel,
        in_specs=[hbm, vmem, vmem],
        out_specs=hbm,
        out_shape=jax.ShapeDtypeStruct((tokens, width), BF16),
        scratch_shapes=[
            pltpu.VMEM((tokens, width), BF16),
            pltpu.SemaphoreType.DMA((tokens // Q,)), pltpu.SemaphoreType.DMA((tokens // Q,)),
        ],
        compiler_params=pltpu.CompilerParams(vmem_limit_bytes=60 * MIB),
        name="norm",
    )(gated, scale, gain)


def on_device(
    inputs, gates, writes, reads, step_raw, step_bias, decay_rate, skip_gain,
    conv_inputs, conv_writes, conv_reads, norm_gain, positions, segments,
    comm=True, phases=5,
):
    tokens, width = inputs.shape
    half_rows = tokens // 2
    n_seq = lax.axis_size("seq") if comm else 16
    n_head = lax.axis_size("head") if comm else 8
    small = (
        writes, reads, step_raw, step_bias[None], decay_rate[None], skip_gain[None],
        conv_inputs, conv_writes, conv_reads, segments.reshape(-1, half_rows // 128, 128),
    )
    gated, scale = main_call(n_seq, n_head, comm, phases, inputs, gates, small, positions)
    return norm_call(gated, scale, norm_gain[None])


def solution(mesh):
    return jax.shard_map(
        on_device,
        mesh=mesh,
        in_specs=(
            P("seq", "head"), P("seq", "head"), P("seq", "head"), P("seq", "head"), P("head", "seq"),
            P("head"), P("head"), P("head"), P(None, "head"), P(None, "head"), P(None, "head"),
            P("head"), P("seq"), P(),
        ),
        out_specs=P("seq", "head"),
        check_vma=False,
    )
```

```python
import functools

import jax
import jax.numpy as jnp
from jax import lax
from jax.experimental import pallas as pl
from jax.experimental.pallas import tpu as pltpu
from jax.sharding import PartitionSpec as P

H = 128
P_SIZE = 128
N = 128
G = 8
Q = 256
SETS = 4
VMEM_MAIN = 60
SCAN_AFTER_SENDING = ((), (), (0,), (1,))
SCAN_AFTER_INNER = {1: (2,), 4: (3,)}
EPSILON = 1e-05
LOG2E = 1.4426950408889634
MESH = pl.DeviceIdType.MESH
MIB = 2**20
F32 = jnp.float32
BF16 = jnp.bfloat16
RIM = 16


def silu_of_half(h):
    return h + h * jnp.tanh(h)


def spread_out(cols, lane, width=P_SIZE):
    return jnp.broadcast_to(cols[:, lane : lane + 1], (cols.shape[0], width))


def main_kernel(
    n_seq, n_head, comm, phases,
    x_hbm, gate_hbm, write_ref, read_ref, step_ref, bias_ref, rate_ref, skip_ref, ci_ref, cw_ref, cr_ref,
    seg_ref, pos_ref,
    out_hbm, scale_ref,
    raw, feats, gate, wct, wc, r_enter, r_half, cols, frow, trow, segs, decay, half_decay, loc_scale, half_scale,
    sloc, state, raw_group, taps, skips, shifts, upper, scores, sq, rim_own, rim_mine, rim_in,
    msg, recv, scanned, back, entering, whole, sums,
    x_sem, g_sem, o_sem, t_sem, h_send, h_recv, s1, r1, s2, r2, s3, r3,
):
    tokens, width = feats.shape
    heads = width // P_SIZE
    chunks = tokens // Q
    per_half = chunks // 2
    half_rows = tokens // 2
    per_set = heads // SETS
    set_width = per_set * P_SIZE
    side = Q // 2
    me = lax.axis_index("seq") if comm else 0
    my_head = lax.axis_index("head") if comm else 0
    slice_rows = N // n_seq
    block = 2 * slice_rows
    states_rows = per_set * block
    CUM, INFO = 0, heads
    first, second = pos_ref[0], pos_ref[half_rows]
    flip = jnp.where(first > second, 1, 0)

    def rows_of(c):
        return pl.ds(pl.multiple_of(c * Q, Q), Q)

    def lanes_of(start, count):
        return pl.ds(pl.multiple_of(start, P_SIZE), count)

    def window_of(c, rim):
        start = c * Q + (c // per_half) * RIM
        return pl.ds(pl.multiple_of(start if rim else start + RIM, RIM), Q + RIM if rim else Q)

    def x_copy(c):
        return pltpu.make_async_copy(x_hbm.at[rows_of(c)], raw.at[window_of(c, False)], x_sem.at[c])

    def gate_copy(c):
        return pltpu.make_async_copy(gate_hbm.at[rows_of(c)], gate.at[rows_of(c)], g_sem.at[c])

    def out_copy(c):
        return pltpu.make_async_copy(feats.at[rows_of(c)], out_hbm.at[rows_of(c)], o_sem.at[c])

    def tail_copy(k):
        end = half_rows * (k + 1)
        return pltpu.make_async_copy(
            x_hbm.at[pl.ds(end - RIM, RIM)], rim_own.at[k, :, pl.ds(0, width)], t_sem.at[k]
        )

    for k in (0, 1):
        tail_copy(k).start()
    for c in range(chunks):
        x_copy(c).start()
    for c in range(chunks):
        gate_copy(c).start()

    if comm:
        barrier = pltpu.get_barrier_semaphore()
        for k in range(1, n_seq):
            pl.semaphore_signal(barrier, inc=1, device_id={"seq": lax.rem(me + k, n_seq)}, device_id_type=MESH)
        for k in range(1, n_head):
            pl.semaphore_signal(barrier, inc=1, device_id={"head": lax.rem(my_head + k, n_head)}, device_id_type=MESH)

    for k in (0, 1):
        tail_copy(k).wait()
        end = half_rows * (k + 1)
        rim_own[k, :, width : width + N] = write_ref[end - RIM : end]
        rim_own[k, :, width + N :] = read_ref[end - RIM : end]
    rim_mine[0] = rim_own[flip]
    rim_mine[1] = rim_own[1 - flip]
    rim_copies = []
    if comm:
        pl.semaphore_wait(barrier, n_seq - 1 + n_head - 1)
        for k, to in ((0, lax.rem(me + 1, n_seq)), (1, lax.rem(me + n_seq - 1, n_seq))):
            rim_copies.append(
                pltpu.make_async_remote_copy(
                    src_ref=rim_mine.at[k], dst_ref=rim_in.at[k], send_sem=h_send.at[k],
                    recv_sem=h_recv.at[k], device_id={"seq": to}, device_id_type=MESH,
                )
            )
            rim_copies[-1].start()

    taps[:, :width] = ci_ref[...].astype(F32) * 0.5
    taps[:, width : width + N] = cw_ref[...].astype(F32) * 0.5
    taps[:, width + N :] = cr_ref[...].astype(F32) * 0.5
    state[...] = jnp.zeros_like(state)
    eye = lax.broadcasted_iota(jnp.int32, (heads, heads), 0) == lax.broadcasted_iota(jnp.int32, (heads, heads), 1)

    def column(ref):
        return jnp.sum(jnp.where(eye, jnp.broadcast_to(ref[...], (heads, heads)), 0.0), axis=1, keepdims=True)

    bias, rate = column(bias_ref), column(rate_ref) * -LOG2E
    skips[...] = jnp.broadcast_to(column(skip_ref), (heads, P_SIZE))
    lane = lax.broadcasted_iota(jnp.int32, (1, half_rows), 1)
    for k, start in ((0, first), (1, second)):
        at = start // half_rows

        def in_a_row(block):
            return jnp.concatenate([block[j : j + 1] for j in range(half_rows // 128)], axis=1).astype(F32)

        here = in_a_row(seg_ref[at])
        ahead = in_a_row(seg_ref[jnp.maximum(at - 1, 0)])
        ahead = jnp.where(jnp.full(ahead.shape, at, jnp.int32) > 0, ahead, -1.0)
        lines = [here]
        for ago in (1, 2, 3):
            lines.append(jnp.where(lane < ago, pltpu.roll(ahead, ago, 1), pltpu.roll(here, ago, 1)))
        for j, line in enumerate(lines):
            segs[j : j + 1, k * half_rows : (k + 1) * half_rows] = line

    row = lax.broadcasted_iota(jnp.int32, (Q, Q), 0)
    col = lax.broadcasted_iota(jnp.int32, (Q, Q), 1)
    upper[...] = jnp.where(row <= col, 1.0, 0.0).astype(F32)

    def by_chunk(one_of):
        return jnp.concatenate([one_of(c) for c in range(chunks)], axis=0)

    def chunk_lanes(c):
        return slice(c * Q, (c + 1) * Q)

    def prepare():
        raw_step = by_chunk(lambda c: step_ref[:, chunk_lanes(c)])
        step = jax.nn.softplus(raw_step + by_chunk(lambda c: bias))
        cum = jnp.dot(
            step * by_chunk(lambda c: rate), upper[...], precision=lax.Precision.HIGHEST, preferred_element_type=F32
        )
        cum_end = cum[:, Q - 1 : Q]
        middle = 0.5 * cum_end
        grown = jnp.exp2(cum - middle)
        factor = jnp.exp2(middle - cum) * step
        tail = jnp.exp2(cum_end - cum) * step
        wide = (heads, 128)
        for c in range(chunks):
            own = slice(c * heads, (c + 1) * heads)
            at = chunk_lanes(c)
            seg, one_ago = segs[0:1, at], segs[1:2, at]
            half_start = (c // per_half) * half_rows
            same = [jnp.where(seg == segs[k : k + 1, at], 1.0, 0.0) for k in (1, 2, 3)]
            enters = jnp.where(seg == one_ago[:, 0:1], 1.0, 0.0)
            enters_half = jnp.where(seg == segs[1:2, half_start : half_start + 1], 1.0, 0.0)
            leaves = jnp.where(seg == seg[:, Q - 1 : Q], 1.0, 0.0)
            base = jnp.zeros((heads, 1), F32) if c % per_half == 0 else base + end
            end, mid = cum_end[own], middle[own]
            frow[c] = factor[own]
            trow[c] = tail[own] * leaves
            decay[c] = jnp.broadcast_to(jnp.exp2(end) * enters[:, Q - 1 : Q], wide)
            half_decay[c] = jnp.broadcast_to(jnp.exp2(base + end) * enters_half[:, Q - 1 : Q], wide)
            loc_scale[c] = jnp.broadcast_to(jnp.exp2(mid), wide)
            half_scale[c] = jnp.broadcast_to(jnp.exp2(base + mid), wide)
            fill = jnp.zeros((128 - heads - 6, Q), F32)
            cols[c * Q : (c + 1) * Q] = jnp.transpose(
                jnp.concatenate([grown[own], seg, *same, enters, enters_half, fill], axis=0)
            )

    if phases >= 1:
        prepare()

    if comm:
        for copy in rim_copies:
            copy.wait()
        rim_in[1] = jnp.where(
            jnp.full(rim_in.shape[1:], me) == n_seq - 1, rim_mine[0].astype(F32), rim_in[1].astype(F32)
        ).astype(BF16)
    for k, rim in ((0, rim_in[flip]), (1, rim_in[1 - flip])):
        start = k * (half_rows + RIM)
        raw[start : start + RIM] = rim[:, :width]
        raw_group[start : start + RIM] = rim[:, width:]
        for j, ref in ((0, write_ref), (1, read_ref)):
            raw_group[start + RIM : start + RIM + half_rows, j * N : (j + 1) * N] = ref[
                k * half_rows : (k + 1) * half_rows
            ]

    to_row = lax.broadcasted_iota(jnp.int32, (side, RIM + side), 0)
    from_row = lax.broadcasted_iota(jnp.int32, (side, RIM + side), 1)

    def conv(source, c, lanes, tap_lanes):
        tap = [taps[k : k + 1, tap_lanes] for k in range(4)]
        x = source[window_of(c, True), lanes]
        out = []
        for b in (0, 1):
            moved = jnp.dot(shifts[2 * c + b], x[b * side : RIM + (b + 1) * side], preferred_element_type=F32)
            total = x[RIM + b * side : RIM + (b + 1) * side].astype(F32) * tap[3]
            for k in (1, 2, 3):
                total = total + moved[(k - 1) * side : k * side] * tap[3 - k]
            out.append(silu_of_half(total))
        return jnp.concatenate(out, axis=0)

    def write_part(c, _):
        info = cols[rows_of(c)]
        for b in (0, 1):
            for k in (1, 2, 3):
                same = spread_out(info[b * side : (b + 1) * side], INFO + k, RIM + side)
                hit = jnp.where(from_row == to_row + (RIM - k), same, 0.0)
                shifts[2 * c + b, (k - 1) * side : k * side] = hit.astype(BF16)
        w = conv(raw_group, c, slice(0, N), slice(width, width + N)).astype(BF16)
        wc[rows_of(c)] = w
        wct[c] = jnp.transpose(w.astype(F32))
        return 0

    if phases >= 2:
        lax.fori_loop(0, chunks, write_part, 0, unroll=4)

    def read_part(c, _):
        info = cols[rows_of(c)]
        r = conv(raw_group, c, slice(N, 2 * N), slice(width + N, width + 2 * N)).astype(BF16)
        wide = r.astype(F32)
        r_enter[rows_of(c)] = (wide * spread_out(info, INFO + 4)).astype(BF16)
        r_half[rows_of(c)] = (wide * spread_out(info, INFO + 5)).astype(BF16)
        full = lax.dot_general(r, wc[rows_of(c)], (((1,), (1,)), ((), ())), preferred_element_type=F32)
        seg_row = segs[0:1, lanes_of(c * Q, Q)]
        keep = (info[:, INFO : INFO + 1] == seg_row) & (col <= row)
        scores[c] = jnp.where(keep, full, 0.0)
        return 0

    def conv_part(g, c, _):
        for pair in range(per_set // 2):
            start = g * set_width + pair * 2 * P_SIZE
            at = slice(start, start + 2 * P_SIZE)
            feats[rows_of(c), at] = conv(raw, c, at, at).astype(BF16)
        return 0

    def state_part(g, c, _):
        half = c // per_half
        w = wct[c]
        for h in range(g * per_set, (g + 1) * per_set):
            one = slice(h, h + 1)
            scaled = (w * trow[c, one, :]).astype(BF16)
            add = jnp.dot(scaled, feats[rows_of(c), h * P_SIZE : (h + 1) * P_SIZE], preferred_element_type=F32)
            old = state[half, h]
            sloc[c, h] = (old * loc_scale[c, one, :]).astype(BF16)
            state[half, h] = old * decay[c, one, :] + add
        return 0

    def state_copy(g, k):
        to = lax.rem(me + k, n_seq)
        return pltpu.make_async_remote_copy(
            src_ref=msg.at[g, to], dst_ref=recv.at[g, me], send_sem=s1.at[g], recv_sem=r1.at[g],
            device_id={"seq": to}, device_id_type=MESH,
        )

    def all_states(g):
        others = pl.ds(0, n_seq - 1)
        return pltpu.make_async_remote_copy(
            src_ref=msg.at[g, others], dst_ref=recv.at[g, others], send_sem=s1.at[g],
            recv_sem=r1.at[g], device_id={"seq": lax.rem(me + 1, n_seq)}, device_id_type=MESH,
        )

    def all_entering(g):
        others = pl.ds(0, n_seq - 1)
        return pltpu.make_async_remote_copy(
            src_ref=back.at[g, others], dst_ref=entering.at[g, others], send_sem=s2.at[g],
            recv_sem=r2.at[g], device_id={"seq": lax.rem(me + 1, n_seq)}, device_id_type=MESH,
        )

    def enter_copy(g, k):
        to = lax.rem(me + k, n_seq)
        return pltpu.make_async_remote_copy(
            src_ref=back.at[g, to], dst_ref=entering.at[g, me], send_sem=s2.at[g], recv_sem=r2.at[g],
            device_id={"seq": to}, device_id_type=MESH,
        )

    def send_states(g):
        decays = []
        for j in range(per_set):
            h = g * per_set + j
            both = []
            for half in (flip, 1 - flip):
                both.append(state[half, h].reshape(n_seq, slice_rows, P_SIZE))
                kept = half_decay[(half + 1) * per_half - 1, h : h + 1]
                high = kept.astype(BF16).astype(F32)
                decays += [high, kept - high]
            msg[g, :, j * block : (j + 1) * block] = jnp.concatenate(both, axis=1).astype(BF16)
        lines = jnp.concatenate(decays, axis=0)
        msg[g, :, states_rows:] = jnp.broadcast_to(lines[None], (n_seq, *lines.shape)).astype(BF16)
        if comm:
            for k in range(1, n_seq):
                state_copy(g, k).start()
            recv[g, me] = msg[g, me]

    def scan_states(g):
        if not comm:
            return
        all_states(g).wait_recv()

        def advance(totals, src, half):
            got = recv[g, src].astype(F32)
            new = []
            for j, total in enumerate(totals):
                at = j * block + half * slice_rows
                scanned[src, at : at + slice_rows] = total
                line = states_rows + 4 * j + 2 * half
                keep = got[line : line + 1] + got[line + 1 : line + 2]
                new.append(total * keep + got[at : at + slice_rows])
            return tuple(new)

        totals = tuple(jnp.zeros((slice_rows, P_SIZE), F32) for _ in range(per_set))
        totals = lax.fori_loop(0, n_seq, lambda k, t: advance(t, k, 0), totals, unroll=4)
        lax.fori_loop(0, n_seq, lambda k, t: advance(t, n_seq - 1 - k, 1), totals, unroll=4)
        back[g] = scanned[...].astype(BF16)
        for k in range(1, n_seq):
            enter_copy(g, k).start()
        entering[g, me] = back[g, me]

    def assemble(g):
        for j in range(per_set):
            h = g * per_set + j
            both = entering[g, :, j * block : (j + 1) * block].astype(F32)
            low = both[:, :slice_rows].reshape(N, P_SIZE)
            high = both[:, slice_rows:].reshape(N, P_SIZE)
            swap = jnp.full(low.shape, flip) > 0
            whole[0, h] = jnp.where(swap, high, low).astype(BF16)
            whole[1, h] = jnp.where(swap, low, high).astype(BF16)

    if phases >= 3:
        for c in range(chunks):
            x_copy(c).wait()
        for g in range(SETS):
            lax.fori_loop(0, chunks, functools.partial(conv_part, g), 0, unroll=4)
            lax.fori_loop(0, chunks, functools.partial(state_part, g), 0, unroll=8)
            send_states(g)
            for ready in SCAN_AFTER_SENDING[g]:
                scan_states(ready)

    def inner_part(c, _):
        info = cols[rows_of(c)]

        masked = scores[c]
        r = r_enter[rows_of(c)]
        for h in range(heads):
            one = slice(h * P_SIZE, (h + 1) * P_SIZE)
            feat = feats[rows_of(c), one]
            fac = frow[c, h : h + 1, :]
            top = jnp.concatenate([r[:side], (masked[:side, :side] * fac[:, :side]).astype(BF16)], axis=1)
            low = jnp.concatenate([r[side:], (masked[side:] * fac).astype(BF16)], axis=1)
            entry = sloc[c, h]
            y = jnp.concatenate(
                [
                    jnp.dot(top, jnp.concatenate([entry, feat[:side]], axis=0), preferred_element_type=F32),
                    jnp.dot(low, jnp.concatenate([entry, feat], axis=0), preferred_element_type=F32),
                ],
                axis=0,
            )
            grown = spread_out(info, CUM + h)
            opened = silu_of_half(gate[rows_of(c), one].astype(F32) * 0.5)
            y = (y * grown + feat.astype(F32) * skips[h : h + 1, :]) * opened
            gate[rows_of(c), one] = (grown * opened).astype(BF16)
            raw[rows_of(c), one] = y.astype(BF16)
        return 0

    if phases >= 4:
        lax.fori_loop(0, chunks, read_part, 0, unroll=4)
        for c in range(chunks):
            gate_copy(c).wait()
        done = 0
        for until, ready in [*SCAN_AFTER_INNER.items(), (chunks, ())]:
            lax.fori_loop(done, until, inner_part, 0)
            done = until
            for g in ready:
                scan_states(g)

    def finish_part(c, _):
        r = r_half[rows_of(c)]
        half = c // per_half
        total = jnp.zeros((Q, P_SIZE), F32)
        for pair in range(heads // 2):
            states = []
            for h in (2 * pair, 2 * pair + 1):
                state_in = whole[half, h].astype(F32)
                states.append((state_in * half_scale[c, h : h + 1, :]).astype(BF16))
            inter = jnp.dot(r, jnp.concatenate(states, axis=1), preferred_element_type=F32)
            for j in (0, 1):
                start = (2 * pair + j) * P_SIZE
                one = slice(start, start + P_SIZE)
                gated = raw[rows_of(c), one].astype(F32)
                gated = gated + inter[:, j * P_SIZE : (j + 1) * P_SIZE] * gate[rows_of(c), one].astype(F32)
                total = total + gated * gated
                feats[rows_of(c), one] = gated.astype(BF16)
        out_copy(c).start()
        sums_here = jnp.sum(jnp.transpose(total), axis=0, keepdims=True)
        sq[c] = jnp.concatenate([sums_here[:, :128], sums_here[:, 128:]], axis=0)
        return 0

    for g in range(SETS):
        if comm:
            all_entering(g).wait_recv()
        assemble(g)

    if phases >= 5:
        lax.fori_loop(0, chunks, finish_part, 0, unroll=2)

    total = sq[...]
    if comm:
        copies = []
        for k in range(1, n_head):
            copies.append(
                pltpu.make_async_remote_copy(
                    src_ref=sq, dst_ref=sums.at[k], send_sem=s3.at[k], recv_sem=r3.at[k],
                    device_id={"head": lax.rem(my_head + k, n_head)}, device_id_type=MESH,
                )
            )
            copies[-1].start()
        for g in range(SETS):
            all_states(g).wait_send()
            all_entering(g).wait_send()
        for k in range(1, n_head):
            copies[k - 1].wait()
            total = total + sums[k]
    scale_ref[...] = lax.rsqrt(total / (H * P_SIZE) + EPSILON)
    if phases >= 5:
        for c in range(chunks):
            out_copy(c).wait()
    if phases < 4:
        for c in range(chunks):
            gate_copy(c).wait()
    if phases < 3:
        for c in range(chunks):
            x_copy(c).wait()


def main_call(n_seq, n_head, comm, phases, inputs, gates, small, positions):
    tokens, width = inputs.shape
    heads = width // P_SIZE
    chunks = tokens // Q
    wide = width + 2 * N
    rows = heads // SETS * 2 * N // n_seq
    vmem = pl.BlockSpec(memory_space=pltpu.VMEM)
    hbm = pl.BlockSpec(memory_space=pl.ANY)
    dma = lambda n: pltpu.SemaphoreType.DMA((n,))
    return pl.pallas_call(
        functools.partial(main_kernel, n_seq, n_head, comm, phases),
        in_specs=[hbm, hbm] + [vmem] * len(small) + [pl.BlockSpec(memory_space=pltpu.SMEM)],
        out_specs=[hbm, vmem],
        out_shape=[
            jax.ShapeDtypeStruct((tokens, width), BF16),
            jax.ShapeDtypeStruct((chunks, Q // 128, 128), F32),
        ],
        scratch_shapes=[
            pltpu.VMEM((tokens + 2 * RIM, width), BF16),
            pltpu.VMEM((tokens, width), BF16),
            pltpu.VMEM((tokens, width), BF16),
            pltpu.VMEM((chunks, N, Q), F32),
            pltpu.VMEM((tokens, N), BF16),
            pltpu.VMEM((tokens, N), BF16),
            pltpu.VMEM((tokens, N), BF16),
            pltpu.VMEM((tokens, 128), F32),
            pltpu.VMEM((chunks, heads, Q), F32),
            pltpu.VMEM((chunks, heads, Q), F32),
            pltpu.VMEM((8, tokens), F32),
            pltpu.VMEM((chunks, heads, 128), F32),
            pltpu.VMEM((chunks, heads, 128), F32),
            pltpu.VMEM((chunks, heads, 128), F32),
            pltpu.VMEM((chunks, heads, 128), F32),
            pltpu.VMEM((chunks, heads, N, P_SIZE), BF16),
            pltpu.VMEM((2, heads, N, P_SIZE), F32),
            pltpu.VMEM((tokens + 2 * RIM, 2 * N), BF16),
            pltpu.VMEM((4, wide), F32),
            pltpu.VMEM((heads, P_SIZE), F32),
            pltpu.VMEM((2 * chunks, 3 * Q // 2, RIM + Q // 2), BF16),
            pltpu.VMEM((Q, Q), F32),
            pltpu.VMEM((chunks, Q, Q), F32),
            pltpu.VMEM((chunks, Q // 128, 128), F32),
            pltpu.VMEM((2, RIM, wide), BF16),
            pltpu.VMEM((2, RIM, wide), BF16),
            pltpu.VMEM((2, RIM, wide), BF16),
            pltpu.VMEM((SETS, n_seq, rows + 4 * heads // SETS, P_SIZE), BF16),
            pltpu.VMEM((SETS, n_seq, rows + 4 * heads // SETS, P_SIZE), BF16),
            pltpu.VMEM((n_seq, rows, P_SIZE), F32),
            pltpu.VMEM((SETS, n_seq, rows, P_SIZE), BF16),
            pltpu.VMEM((SETS, n_seq, rows, P_SIZE), BF16),
            pltpu.VMEM((2, heads, N, P_SIZE), BF16),
            pltpu.VMEM((n_head, chunks, Q // 128, 128), F32),
            dma(chunks), dma(chunks), dma(chunks), dma(2), dma(2), dma(2),
            *[dma(SETS)] * 4, dma(n_head), dma(n_head),
        ],
        compiler_params=pltpu.CompilerParams(
            vmem_limit_bytes=VMEM_MAIN * MIB,
            **(dict(collective_id=0, has_side_effects=True) if comm else {}),
        ),
        name="main",
    )(inputs, gates, *small, positions)


def norm_kernel(gated_hbm, scale_ref, gain_ref, out_hbm, rows, in_sem, out_sem):
    chunks = scale_ref.shape[0]

    def part(c):
        return pl.ds(c * Q, Q)

    def in_copy(c):
        return pltpu.make_async_copy(gated_hbm.at[part(c)], rows.at[part(c)], in_sem.at[c])

    def out_copy(c):
        return pltpu.make_async_copy(rows.at[part(c)], out_hbm.at[part(c)], out_sem.at[c])

    for c in range(chunks):
        in_copy(c).start()
    for c in range(chunks):
        scale = scale_ref[c]
        line = jnp.concatenate([scale[0:1], scale[1:2]], axis=1)
        col = jnp.transpose(jnp.broadcast_to(line, (128, Q)))
        in_copy(c).wait()
        for k in range(rows.shape[1] // 128):
            at = slice(k * 128, (k + 1) * 128)
            rows[part(c), at] = (rows[part(c), at].astype(F32) * col * gain_ref[:, at]).astype(BF16)
        out_copy(c).start()
    for c in range(chunks):
        out_copy(c).wait()


def norm_call(gated, scale, gain):
    tokens, width = gated.shape
    vmem = pl.BlockSpec(memory_space=pltpu.VMEM)
    hbm = pl.BlockSpec(memory_space=pl.ANY)
    return pl.pallas_call(
        norm_kernel,
        in_specs=[hbm, vmem, vmem],
        out_specs=hbm,
        out_shape=jax.ShapeDtypeStruct((tokens, width), BF16),
        scratch_shapes=[
            pltpu.VMEM((tokens, width), BF16),
            pltpu.SemaphoreType.DMA((tokens // Q,)), pltpu.SemaphoreType.DMA((tokens // Q,)),
        ],
        compiler_params=pltpu.CompilerParams(vmem_limit_bytes=60 * MIB),
        name="norm",
    )(gated, scale, gain)


def on_device(
    inputs, gates, writes, reads, step_raw, step_bias, decay_rate, skip_gain,
    conv_inputs, conv_writes, conv_reads, norm_gain, positions, segments,
    comm=True, phases=5,
):
    tokens, width = inputs.shape
    half_rows = tokens // 2
    n_seq = lax.axis_size("seq") if comm else 16
    n_head = lax.axis_size("head") if comm else 8
    small = (
        writes, reads, step_raw, step_bias[None], decay_rate[None], skip_gain[None],
        conv_inputs, conv_writes, conv_reads, segments.reshape(-1, half_rows // 128, 128),
    )
    gated, scale = main_call(n_seq, n_head, comm, phases, inputs, gates, small, positions)
    return norm_call(gated, scale, norm_gain[None])


def solution(mesh):
    return jax.shard_map(
        on_device,
        mesh=mesh,
        in_specs=(
            P("seq", "head"), P("seq", "head"), P("seq", "head"), P("seq", "head"), P("head", "seq"),
            P("head"), P("head"), P("head"), P(None, "head"), P(None, "head"), P(None, "head"),
            P("head"), P("seq"), P(),
        ),
        out_specs=P("seq", "head"),
        check_vma=False,
    )
```
